32 devices in a mesh: grp: 4 (over y, x), dev: 8 (over z, core).
Axes of the slice: x: 2, y: 2, z: 4, core: 2. Of those that a mesh axis runs over, the one named last changes fastest.
Arguments:
- child_weights: float32 [2, 256, 4, 64, 64], P(None, ('grp', 'dev')), may hold values from -0.12 to 0.12
- pivots: int32 [256, 32], P(('grp', 'dev')), may hold values from 0 to 1023, as said below
- ranks: int32 [256], replicated, may hold values from 1 to 32, 2560 in all
- owner_slot: int32 [256], replicated, may hold values from 0 to 255, each once
Outputs:
- skeleton_sums: float32 [2, 32, 256, 64], P(None, None, ('grp', 'dev'))
The draws below stay inside these ranges and needn't reach their ends.
Inputs may be any that keep to these rules, and one draw needn't show every extreme that they name: `pivots`: each row lists 32 distinct points of one target box, numbered row by row within the box. The ranks sum to 2560; some box has rank 32. A permutation: box a is owned by device floor(owner_slot[a] / 8) of grp+dev, at place owner_slot[a] mod 8.
All inputs are finite; a program needn't handle non-finite values.
Results may differ from the reference program's by a relative error of at most 0.0003.
Values sent between devices are 32-bit elements; how exact they have to be, the bound alone decides.
A program may use at most 64 MiB of HBM per device.

```python
import math
import jax
import jax.numpy as jnp
import numpy as np
from jax import lax

GRID = 2048
Q = 8
R = 64
RT = 32
RMEAN = 10
NSB = 256
NA = 256
NAP = 64
NP = 64


def draw_pivots(key, part):
    points = GRID * GRID // 4096
    key_scores, key_high, key_low = jax.random.split(key, 3)
    scores = jax.random.randint(key_scores, (NA, points), 0, 1 << 20, dtype=jnp.int32) * points + jnp.arange(points, dtype=jnp.int32)[None, :]
    high_box = jax.random.randint(key_high, (), 0, NA, dtype=jnp.int32)
    low_box = jax.random.randint(key_low, (), 0, NA, dtype=jnp.int32)
    row_ids = jnp.arange(NA, dtype=jnp.int32)[:, None]
    col_ids = jnp.arange(points, dtype=jnp.int32)[None, :]
    scores = jnp.where((row_ids == high_box) & (col_ids == points - 1), -2, scores)
    scores = jnp.where((row_ids == low_box) & (col_ids == 0), -1, scores)
    ranked = jnp.argsort(scores, axis=1, stable=True)
    return ranked[:, :RT].astype(jnp.int32)


def block_levels(rng, shape, cuts, least, largest):
    def one(position, parts):
        heights = jax.random.uniform(jax.random.fold_in(jax.random.fold_in(rng, 6), position), (parts,), jnp.float32, least / len(cuts), largest / len(cuts))
        return jnp.repeat(jnp.exp(heights), shape[position] // parts).reshape((-1,) + (1,) * (len(shape) - position - 1))

    factor_of = one(*cuts[0])
    for cut in cuts[1:]:
        factor_of = factor_of * one(*cut)
    return factor_of


def length_profile(count, total, most, lean):
    portions = [(1 << 20) // math.isqrt(grade ** lean) + 1 for grade in range(2, count + 1)]
    spare, holding = total - most - (count - 1), [1] * (count - 1)
    while spare > 0:
        candidates = [i for i in range(count - 1) if holding[i] < most]
        whole, left = sum([portions[i] for i in candidates]), spare
        for i in candidates:
            more = min(most - holding[i], max(1, left * portions[i] // whole), spare)
            holding[i] = holding[i] + more
            spare = spare - more
    return np.array([most] + holding)


def ragged_sizes(own_key, amount, total, reach, lean):
    if amount == 2:
        one = jax.random.randint(own_key, (), max(1, total - reach), min(reach, total - 1) + 1)
        return jnp.stack([one, total - one])
    lengths = jnp.asarray(length_profile(amount, total, reach, lean), jnp.int32)
    pairs = (amount - 1) // 2
    donor, taker = lengths[1:1 + 2 * pairs:2], lengths[2:2 + 2 * pairs:2]
    room = jnp.minimum(donor - 1, reach - taker)
    shifted = jax.random.randint(jax.random.fold_in(own_key, 1), (pairs,), 0, 1 << 20) % (room + 1)
    lengths = lengths.at[1:1 + 2 * pairs:2].set(donor - shifted).at[2:2 + 2 * pairs:2].set(taker + shifted)
    return lengths[jax.random.permutation(jax.random.fold_in(own_key, 2), amount)]


def centred(stream_key, shape, scale, limit, cuts=(), held_as=jnp.bfloat16):
    values = scale * jax.random.normal(stream_key, shape, jnp.float32)
    if cuts:
        values = values * block_levels(stream_key, shape, cuts, -0.22, 0.18)
    return jnp.clip(values, -limit, limit).astype(held_as)


def setup_inputs(seed: int = 0) -> dict:
    keys = jax.random.split(jax.random.key(seed), 5)
    return {
        "child_weights": centred(keys[0], (2, NSB, 4, R, NAP), 0.02, 0.12, ((1, 32),), jnp.float32),
        "pivots": draw_pivots(jax.random.fold_in(keys[4], 71), 0),
        "ranks": ragged_sizes(keys[2], NA, NA * RMEAN, RT, 2).astype(jnp.int32),
        "owner_slot": jax.random.permutation(keys[3], NA).astype(jnp.int32),
    }


TWO_PI = 2.0 * math.pi
speed_waves = 8

def cheb_nodes(degree):
    steps_j = jnp.arange(degree, dtype=jnp.float32)
    return jnp.cos(math.pi * (2.0 * steps_j + 1.0) / (2.0 * degree))

def lagrange_table(nodes_at, points):
    degree = nodes_at.shape[0]
    differ = points[None, :] - nodes_at[:, None]
    diagonal_mask = jnp.eye(degree, dtype=bool)
    factors = jnp.where(diagonal_mask[:, :, None], 1.0, differ[None, :, :])
    numerator = jnp.prod(factors, axis=1)
    node_gaps = nodes_at[:, None] - nodes_at[None, :] + jnp.eye(degree, dtype=nodes_at.dtype)
    return numerator / jnp.prod(node_gaps, axis=1)[:, None]

def child_table(degree):
    chebyshev = cheb_nodes(degree)
    halves = jnp.stack([lagrange_table(chebyshev, child_side - 0.5 + 0.5 * chebyshev) for child_side in (0.0, 1.0)])
    interp_table = jnp.einsum('uaj,vbk->abuvjk', halves, halves)
    return interp_table.reshape(degree * degree, 4 * degree * degree)

def proxy_offsets(degree, grid_cells):
    chebyshev = cheb_nodes(degree)
    source_side = grid_cells // 32
    quarter = source_side / 4.0
    child_half = jnp.arange(2, dtype=jnp.float32) * (source_side / 2.0)
    along = child_half[:, None] + (quarter - 0.5) + quarter * chebyshev[None, :]
    child_x = jnp.broadcast_to(along[:, None, :, None], (2, 2, degree, degree)).reshape(-1)
    child_y = jnp.broadcast_to(along[None, :, None, :], (2, 2, degree, degree)).reshape(-1)
    parent_along = source_side / 2.0 - 0.5 + source_side / 2.0 * chebyshev
    parent_x = jnp.broadcast_to(parent_along[:, None], (degree, degree)).reshape(-1)
    parent_y = jnp.broadcast_to(parent_along[None, :], (degree, degree)).reshape(-1)
    return (child_x, child_y, parent_x, parent_y)

def phase_cycles(head_x, head_y, denominator, corner_x, corner_y, shift_x, shift_y):
    whole_part = jnp.mod(head_x * corner_x + head_y * corner_y, denominator).astype(jnp.float32) / denominator
    place_x = head_x.astype(jnp.float32) / denominator
    place_y = head_y.astype(jnp.float32) / denominator
    turn_x = TWO_PI * jnp.mod(speed_waves * head_x, denominator).astype(jnp.float32) / denominator
    turn_y = TWO_PI * jnp.mod(speed_waves * head_y, denominator).astype(jnp.float32) / denominator
    speed_x = (2.0 + jnp.sin(turn_x) * jnp.sin(turn_y)) / 16.0
    speed_y = (2.0 + jnp.cos(turn_x) * jnp.cos(turn_y)) / 16.0
    freq_x = corner_x.astype(jnp.float32) + shift_x
    freq_y = corner_y.astype(jnp.float32) + shift_y
    return whole_part + place_x * shift_x + place_y * shift_y + jnp.sqrt((speed_x * freq_x) ** 2 + (speed_y * freq_y) ** 2)

def target_centres(box_ids, grid_cells):
    target_side = grid_cells // 64
    target_row = grid_cells // 32
    return (2 * (box_ids // target_row) * target_side + target_side - 1, 2 * (box_ids % target_row) * target_side + target_side - 1)

def pivot_points(box_ids, pivot_ids, grid_cells):
    target_side = grid_cells // 64
    target_row = grid_cells // 32
    return (box_ids // target_row * target_side + pivot_ids // target_side, box_ids % target_row * target_side + pivot_ids % target_side)

def source_box(child_box, box_id, centre_x, centre_y, offsets, interp_table, grid_cells):
    child_x, child_y, parent_x, parent_y = offsets
    corner_x = box_id // (grid_cells // 64) * (grid_cells // 32) - grid_cells // 2
    corner_y = box_id % (grid_cells // 64) * (grid_cells // 32) - grid_cells // 2
    half_row = grid_cells // 64
    inner = child_box.shape[1]
    parents = child_box.shape[2]
    spread = child_box.reshape(2, inner, parents // half_row, 1, half_row, 1)
    spread = jnp.broadcast_to(spread, (2, inner, parents // half_row, 2, half_row, 2)).reshape(2, inner, 4 * parents)
    phase_now = TWO_PI * phase_cycles(centre_x[None, :], centre_y[None, :], 2 * grid_cells, corner_x, corner_y, child_x[:, None], child_y[:, None])
    cosine = jnp.cos(phase_now)
    sine_part = jnp.sin(phase_now)
    stacked = jnp.stack([spread[0] * cosine + spread[1] * sine_part, spread[1] * cosine - spread[0] * sine_part])
    interp = jnp.einsum('tc,zca->zta', interp_table, stacked, precision=lax.Precision.HIGHEST)
    phase_back = TWO_PI * phase_cycles(centre_x[None, :], centre_y[None, :], 2 * grid_cells, corner_x, corner_y, parent_x[:, None], parent_y[:, None])
    cosine_back = jnp.cos(phase_back)
    sine_back = jnp.sin(phase_back)
    return jnp.stack([interp[0] * cosine_back - interp[1] * sine_back, interp[0] * sine_back + interp[1] * cosine_back])

def skeleton_rows(point_x, point_y, box_ids, weights, offsets, grid_cells):
    parent_x = offsets[2]
    parent_y = offsets[3]
    corner_x = box_ids // (grid_cells // 64) * (grid_cells // 32) - grid_cells // 2
    corner_y = box_ids % (grid_cells // 64) * (grid_cells // 32) - grid_cells // 2
    phase_now = TWO_PI * phase_cycles(point_x[None, None, :], point_y[None, None, :], grid_cells, corner_x[:, None, None], corner_y[:, None, None], parent_x[None, :, None], parent_y[None, :, None])
    cosine = jnp.cos(phase_now)
    sine_part = jnp.sin(phase_now)
    real_sum = lax.optimization_barrier(jnp.sum(cosine * weights[:, 0] - sine_part * weights[:, 1], axis=1))
    imag_sum = lax.optimization_barrier(jnp.sum(sine_part * weights[:, 0] + cosine * weights[:, 1], axis=1))
    return jnp.stack([real_sum, imag_sum])

def reference(child_weights, pivots, ranks, owner_slot):
    grid_cells = GRID
    interp_table = child_table(Q)
    offsets = proxy_offsets(Q, grid_cells)
    targets_all = jnp.arange(NA, dtype=jnp.int32)
    centre_x, centre_y = target_centres(targets_all, grid_cells)

    def one_box(box_id):
        child_box = lax.dynamic_index_in_dim(child_weights, box_id, 1, keepdims=False).reshape(2, 4 * Q * Q, NA // 4)
        return source_box(child_box, box_id, centre_x, centre_y, offsets, interp_table, grid_cells)
    weights = lax.map(one_box, jnp.arange(NSB, dtype=jnp.int32))
    live_total = NA * RMEAN
    rank_ends = jnp.cumsum(ranks).astype(jnp.int32)
    starts = rank_ends - ranks
    live_rows = jnp.arange(live_total, dtype=jnp.int32)
    live_box = jnp.searchsorted(rank_ends, live_rows, side='right').astype(jnp.int32)
    live_rank = live_rows - starts[live_box]
    live_pivot = pivots[live_box, live_rank]
    point_x, point_y = pivot_points(live_box, live_pivot, grid_cells)
    block_rows = math.gcd(live_total, 256)
    box_ids = jnp.arange(NSB, dtype=jnp.int32)

    def one_block(block_args):
        box_block, x_block, y_block = block_args
        gathered = jnp.take(weights, box_block, axis=3)
        return skeleton_rows(x_block, y_block, box_ids, gathered, offsets, grid_cells)
    block_parts = lax.map(one_block, (live_box.reshape(-1, block_rows), point_x.reshape(-1, block_rows), point_y.reshape(-1, block_rows)))
    live_values = jnp.moveaxis(block_parts, 0, 2).reshape(2, NSB, live_total)
    slot_box = jnp.argsort(owner_slot).astype(jnp.int32)
    rank_ids = jnp.arange(RT, dtype=jnp.int32)
    padded_index = jnp.minimum(starts[slot_box][None, :] + rank_ids[:, None], live_total - 1)
    valid_rows = rank_ids[:, None] < ranks[slot_box][None, :]
    padded = jnp.where(valid_rows[None, None], live_values[:, :, padded_index], 0.0)
    grouped = padded.reshape(2, NSB // 64, 2, grid_cells // 128, 2, RT, NA).sum(axis=(2, 4))
    grouped = grouped.reshape(2, NP, RT, NA)
    return jnp.transpose(grouped, (0, 2, 3, 1))
```

```python
import math

import jax
import jax.numpy as jnp
import numpy as np
from jax import lax
from jax.experimental import pallas as pl
from jax.experimental.pallas import tpu as pltpu
from jax.sharding import PartitionSpec as P

GRID = 2048
Q = 8
RT = 32
RMEAN = 10
SIDE = GRID // 32
WIDTH = GRID // 64
ROW = GRID // 64
COLS = GRID // 32
LANES = 128
R = Q * Q

SIN = (4.442867904603554, -7.30744348201647, 3.594788644821573, -0.7843755040132807)
COS = (1.414213496570567, -6.978850989042699, 5.73946118893746, -1.883563117820809, 0.31069847934250466)

F32 = jnp.float32
BF16 = jnp.bfloat16


def nodes():
    return np.cos(np.pi * (2.0 * np.arange(Q) + 1.0) / (2.0 * Q))


def lagrange(at, points):
    out = np.ones((Q, Q))
    for t in range(Q):
        for k in range(Q):
            if k != t:
                out[t] *= (points - at[k]) / (at[t] - at[k])
    return out


def child_table():
    c = nodes()
    halves = np.stack([lagrange(c, u - 0.5 + 0.5 * c) for u in (0.0, 1.0)])
    return np.einsum("uaj,vbk->abuvjk", halves, halves).reshape(R, 4 * R)


def split_table():
    table = child_table().astype(np.float32)
    high = table.astype(jnp.bfloat16)
    low = (table - high.astype(np.float32)).astype(jnp.bfloat16)
    return np.concatenate([high, low, high], axis=1)


def offsets():
    c = nodes()
    parent = SIDE / 2 - 0.5 + SIDE / 2 * c
    child = np.concatenate([SIDE * u / 2 + SIDE / 4 - 0.5 + SIDE / 4 * c for u in (0, 1)])
    return child, parent


def centre_rows(targets):
    a = np.arange(targets)
    x1 = (2 * WIDTH * (a // COLS) + WIDTH - 1) / (2 * GRID)
    x2 = (2 * WIDTH * (a % COLS) + WIDTH - 1) / (2 * GRID)
    c1 = (2 + np.sin(16 * np.pi * x1) * np.sin(16 * np.pi * x2)) / 16
    c2 = (2 + np.cos(16 * np.pi * x1) * np.cos(16 * np.pi * x2)) / 16
    child, parent = offsets()
    rows = [np.stack([c1, c2] + [np.zeros(targets)] * 6)]
    for o in (child, parent):
        for x in (x1, x2):
            turn = o[:, None] * x[None, :]
            rows.append(turn - np.floor(turn))
    return np.concatenate(rows).astype(np.float32)


def offset_columns():
    child, parent = offsets()
    return np.broadcast_to(np.concatenate([child, parent])[:, None], (3 * Q, LANES)).astype(np.float32)


def half_turn(phase):
    r = phase - jnp.round(phase)
    q = r * r
    s = SIN[3]
    for coefficient in SIN[2::-1]:
        s = s * q + coefficient
    s = s * r
    c = COS[4]
    for coefficient in COS[3::-1]:
        c = c * q + coefficient
    return s * s, s * c


def root(square):
    return jnp.sqrt(square)


def corner(own_boxes, box):
    position = lax.axis_index("grp") * lax.axis_size("dev") + lax.axis_index("dev")
    box_id = position * own_boxes + box
    return (box_id // ROW) * SIDE - GRID // 2, (box_id % ROW) * SIDE - GRID // 2


def outer(column, tile):
    return jnp.concatenate([column[j : j + 1] + tile for j in range(Q)], axis=0)


def source_kernel(own_boxes, targets, parents, weights_ref, table_ref, centre_ref, offset_ref, delta_ref):
    k1, k2 = corner(own_boxes, pl.program_id(0))
    k1f, k2f = k1.astype(F32), k2.astype(F32)
    offs = offset_ref[...]
    for g in range(targets // LANES):
        lanes = slice(g * LANES, (g + 1) * LANES)
        lane = lax.broadcasted_iota(jnp.int32, (1, LANES), 1)
        box = lane + g * LANES
        h1 = 2 * WIDTH * (box // COLS) + WIDTH - 1
        h2 = 2 * WIDTH * (box % COLS) + WIDTH - 1
        whole = ((h1 * k1 + h2 * k2) & (2 * GRID - 1)).astype(F32) * (1.0 / (2 * GRID))
        c1 = centre_ref[0:1, lanes]
        c2 = centre_ref[1:2, lanes]
        first = c1 * (k1f + offs)
        first = first * first
        second = c2 * (k2f + offs)
        second = second * second
        turn1 = centre_ref[8 : 8 + 2 * Q, lanes]
        turn2 = centre_ref[8 + 2 * Q : 8 + 4 * Q, lanes] + whole
        back1 = centre_ref[8 + 4 * Q : 8 + 5 * Q, lanes]
        back2 = centre_ref[8 + 5 * Q : 8 + 6 * Q, lanes] + whole
        parent_lane = (g * (COLS // 2)) % LANES + (lane % COLS) // 2
        pick = jnp.broadcast_to(parent_lane, (R, LANES))
        start = (g * (COLS // 2)) // LANES * LANES
        high, low = [], []
        for u in range(2):
            for v in range(2):
                one, two = slice(u * Q, (u + 1) * Q), slice(v * Q, (v + 1) * Q)
                phase = root(outer(first[one], second[two])) + outer(turn1[one], turn2[two])
                less, sine = half_turn(phase)
                spread = []
                for z in range(2):
                    w = weights_ref[z, 0, 2 * u + v, :, start : min(start + LANES, parents)]
                    if w.shape[1] < LANES:
                        w = jnp.concatenate([w] * (LANES // w.shape[1]), axis=1)
                    spread.append(jnp.take_along_axis(w, pick, axis=1, mode="promise_in_bounds"))
                wr, wi = spread
                both = jnp.concatenate(
                    [wr - (wr * less - wi * sine), wi - (wi * less + wr * sine)], axis=1
                )
                top = both.astype(BF16)
                high.append(top)
                low.append((both - top.astype(F32)).astype(BF16))
        moved = jnp.concatenate(high + high + low, axis=0)
        interp = jnp.dot(table_ref[...], moved, preferred_element_type=F32)
        ir, ii = interp[:, :LANES], interp[:, LANES:]
        parent = slice(2 * Q, 3 * Q)
        phase = root(outer(first[parent], second[parent])) + outer(back1, back2)
        less, sine = half_turn(phase)
        for z, part in enumerate((ir - (ir * less + ii * sine), ii - (ii * less - ir * sine))):
            top = part.astype(BF16)
            delta_ref[0, z, :, lanes] = top
            delta_ref[0, z, :, targets + g * LANES : targets + (g + 1) * LANES] = (
                part - top.astype(F32)
            ).astype(BF16)


def skeleton_kernel(
    own_boxes, targets, begin_ref, delta_ref, facts_ref, range_ref, place_ref, offset_ref, out_ref, picked, compact
):
    chunks = targets * RMEAN // LANES
    offs = offset_ref[2 * Q : 3 * Q]
    firsts = range_ref[0:1]
    ends = range_ref[1:2]
    corners = [corner(own_boxes, b) for b in range(own_boxes)]
    ranks_down = lax.broadcasted_iota(jnp.int32, (RT, LANES), 0)

    def one_chunk(c, carry):
        row = lax.broadcasted_iota(jnp.int32, (LANES, targets), 0) + c * LANES
        hot = jnp.where((firsts <= row) & (row < ends), 1.0, 0.0).astype(BF16)
        contract = (((1,), (1,)), ((), ()))
        facts = lax.dot_general(facts_ref[...], hot, contract, preferred_element_type=F32)
        picked[...] = lax.dot_general(
            delta_ref[...], jnp.concatenate([hot, hot], axis=1), contract, preferred_element_type=F32
        )
        facts = facts.astype(jnp.int32)
        here = lax.broadcasted_iota(jnp.int32, (1, LANES), 1) + c * LANES
        rank = here - (facts[2 * RT + 2 : 2 * RT + 3] * LANES + facts[2 * RT + 3 : 2 * RT + 4])
        mine = ranks_down == rank
        p1 = jnp.sum(jnp.where(mine, facts[:RT], 0), axis=0, keepdims=True)
        p2 = jnp.sum(jnp.where(mine, facts[RT : 2 * RT], 0), axis=0, keepdims=True)
        h1 = facts[2 * RT : 2 * RT + 1] * WIDTH + p1
        h2 = facts[2 * RT + 1 : 2 * RT + 2] * WIDTH + p2
        x1 = h1.astype(F32) * (1.0 / GRID)
        x2 = h2.astype(F32) * (1.0 / GRID)
        angle = jnp.concatenate([h1, h2], axis=0)
        angle = ((8 * angle) & (GRID - 1)).astype(F32) * (2.0 * math.pi / GRID)
        sines, cosines = jnp.sin(angle), jnp.cos(angle)
        c1 = (2.0 + sines[0:1] * sines[1:2]) * (1.0 / 16)
        c2 = (2.0 + cosines[0:1] * cosines[1:2]) * (1.0 / 16)
        turn1 = x1 * offs
        turn1 = turn1 - jnp.floor(turn1)
        turn2 = x2 * offs
        turn2 = turn2 - jnp.floor(turn2)
        first = c1 * (corners[0][0].astype(F32) + offs)
        first = first * first
        sums = []
        for b, (k1, k2) in enumerate(corners):
            whole = ((h1 * k1 + h2 * k2) & (GRID - 1)).astype(F32) * (1.0 / GRID)
            second = c2 * (k2.astype(F32) + offs)
            second = second * second
            phase = root(outer(first, second)) + outer(turn1, turn2 + whole)
            less, sine = half_turn(phase)
            wr = picked[2 * b * R : (2 * b + 1) * R]
            wi = picked[(2 * b + 1) * R : (2 * b + 2) * R]
            real = wr - (wr * less + wi * sine)
            imag = wi - (wi * less - wr * sine)
            sums.append((jnp.sum(real.reshape(Q, Q, LANES), axis=0), jnp.sum(imag.reshape(Q, Q, LANES), axis=0)))
        rows = [
            jnp.sum(sums[b][z] + sums[b + 1][z], axis=0, keepdims=True)
            for z in range(2)
            for b in range(0, own_boxes, 2)
        ]
        compact[c] = jnp.concatenate(rows, axis=0)
        return carry

    lax.fori_loop(0, chunks, one_chunk, 0)
    compact[chunks] = jnp.zeros_like(compact[0])
    boxes = LANES // RT

    def one_place(n, carry):
        chunk = begin_ref[n * boxes] // LANES
        place = jnp.broadcast_to(place_ref[pl.ds(n, 1)], (own_boxes, LANES))
        local = place - chunk * LANES
        within = local & (LANES - 1)
        near = jnp.take_along_axis(compact[chunk], within, axis=1, mode="promise_in_bounds")
        far = jnp.take_along_axis(compact[chunk + 1], within, axis=1, mode="promise_in_bounds")
        out_ref[n] = jnp.where(place < 0, 0.0, jnp.where(local >= LANES, far, near))
        return carry

    lax.fori_loop(0, targets // boxes, one_place, 0, unroll=4)


def local(child_weights, pivots, ranks, owner_slot):
    group_size = lax.axis_size("grp") * lax.axis_size("dev")
    own_boxes = child_weights.shape[1]
    parents = child_weights.shape[4]
    targets = ranks.shape[0]
    per_owner = targets // group_size
    vmem = pl.BlockSpec(memory_space=pltpu.VMEM)
    smem = pl.BlockSpec(memory_space=pltpu.SMEM)

    all_pivots = lax.all_gather(pivots, ("grp", "dev"), axis=0, tiled=True)
    offs = offset_columns()
    centre = centre_rows(targets)
    delta = pl.pallas_call(
        lambda *refs: source_kernel(own_boxes, targets, parents, *refs),
        grid=(own_boxes,),
        in_specs=[
            pl.BlockSpec((2, 1, 4, R, parents), lambda b: (0, b, 0, 0, 0)),
            pl.BlockSpec((R, 12 * R), lambda b: (0, 0)),
            pl.BlockSpec(centre.shape, lambda b: (0, 0)),
            pl.BlockSpec(offs.shape, lambda b: (0, 0)),
        ],
        out_specs=pl.BlockSpec((1, 2, R, 2 * targets), lambda b: (b, 0, 0, 0)),
        out_shape=jax.ShapeDtypeStruct((own_boxes, 2, R, 2 * targets), BF16),
        compiler_params=pltpu.CompilerParams(vmem_limit_bytes=48 << 20),
        cost_estimate=pl.CostEstimate(flops=200_000_000, bytes_accessed=4_000_000, transcendentals=0),
    )(child_weights, split_table(), centre, offs)

    ids = jnp.arange(targets, dtype=jnp.int32)
    starts = jnp.sum(jnp.where(owner_slot[:, None] < owner_slot[None, :], ranks[:, None], 0), axis=0)
    begin = jnp.sum(jnp.where(owner_slot[:, None] < ids[None, :], ranks[:, None], 0), axis=0)
    count = jnp.sum(jnp.where(owner_slot[:, None] == ids[None, :], ranks[:, None], 0), axis=0)
    ranges = jnp.stack([starts, starts + ranks])
    columns = all_pivots.T
    facts = jnp.concatenate(
        [columns // WIDTH, columns % WIDTH]
        + [row[None] for row in (ids // COLS, ids % COLS, starts // LANES, starts % LANES)]
        + [jnp.zeros((12, targets), jnp.int32)]
    ).astype(BF16)
    rank_ids = jnp.arange(RT, dtype=jnp.int32)
    place = jnp.where(rank_ids[None] < count[:, None], begin[:, None] + rank_ids[None], -1)
    place = place.reshape(-1, LANES)
    chunks = targets * RMEAN // LANES
    rows = pl.pallas_call(
        lambda *refs: skeleton_kernel(own_boxes, targets, *refs),
        in_specs=[smem, vmem, vmem, vmem, vmem, vmem],
        out_specs=vmem,
        out_shape=jax.ShapeDtypeStruct((place.shape[0], own_boxes, LANES), F32),
        scratch_shapes=[
            pltpu.VMEM((own_boxes * 2 * R, LANES), F32),
            pltpu.VMEM((chunks + 1, own_boxes, LANES), F32),
        ],
        compiler_params=pltpu.CompilerParams(vmem_limit_bytes=48 << 20),
    )(begin, delta.reshape(own_boxes * 2 * R, 2 * targets), facts, ranges, place, offs)

    received = lax.all_to_all(rows, ("grp", "dev"), split_axis=0, concat_axis=0, tiled=True)
    halves = own_boxes // 2
    pair = ROW // own_boxes
    received = received.reshape(group_size // (2 * pair), 2, pair, per_owner * RT // LANES, 2, halves, LANES // RT, RT)
    summed = received[:, 0] + received[:, 1]
    result = jnp.transpose(summed, (3, 6, 2, 5, 0, 1, 4))
    return result.reshape(2, RT, per_owner, group_size * own_boxes // 4)


def solution(mesh):
    in_specs = (P(None, ("grp", "dev"), None, None, None), P(("grp", "dev"), None), P(), P())
    out_specs = P(None, None, ("grp", "dev"), None)
    return jax.shard_map(local, mesh=mesh, in_specs=in_specs, out_specs=out_specs, check_vma=False)
```

```python
import math

import jax
import jax.numpy as jnp
import numpy as np
from jax import lax
from jax.experimental import pallas as pl
from jax.experimental.pallas import tpu as pltpu
from jax.sharding import PartitionSpec as P

GRID = 2048
Q = 8
RT = 32
RMEAN = 10
SIDE = GRID // 32
WIDTH = GRID // 64
ROW = GRID // 64
COLS = GRID // 32
LANES = 128
R = Q * Q

SIN = (4.442867904603554, -7.30744348201647, 3.594788644821573, -0.7843755040132807)
COS = (1.414204082132758, -6.977642209183305, 5.715240371096478, -1.7283548501332477)

F32 = jnp.float32
BF16 = jnp.bfloat16


def nodes():
    return np.cos(np.pi * (2.0 * np.arange(Q) + 1.0) / (2.0 * Q))


def lagrange(at, points):
    out = np.ones((Q, Q))
    for t in range(Q):
        for k in range(Q):
            if k != t:
                out[t] *= (points - at[k]) / (at[t] - at[k])
    return out


def child_table():
    c = nodes()
    halves = np.stack([lagrange(c, u - 0.5 + 0.5 * c) for u in (0.0, 1.0)])
    return np.einsum("uaj,vbk->abuvjk", halves, halves).reshape(R, 4 * R)


def split_table():
    table = child_table().astype(np.float32)
    high = table.astype(jnp.bfloat16)
    low = (table - high.astype(np.float32)).astype(jnp.bfloat16)
    return np.concatenate([high, low, high], axis=1)


def offsets():
    c = nodes()
    parent = SIDE / 2 - 0.5 + SIDE / 2 * c
    child = np.concatenate([SIDE * u / 2 + SIDE / 4 - 0.5 + SIDE / 4 * c for u in (0, 1)])
    return child, parent


def centre_rows(targets):
    a = np.arange(targets)
    x1 = (2 * WIDTH * (a // COLS) + WIDTH - 1) / (2 * GRID)
    x2 = (2 * WIDTH * (a % COLS) + WIDTH - 1) / (2 * GRID)
    c1 = (2 + np.sin(16 * np.pi * x1) * np.sin(16 * np.pi * x2)) / 16
    c2 = (2 + np.cos(16 * np.pi * x1) * np.cos(16 * np.pi * x2)) / 16
    child, parent = offsets()
    rows = [np.stack([c1, c2] + [np.zeros(targets)] * 6)]
    for o in (child, parent):
        for x in (x1, x2):
            turn = o[:, None] * x[None, :]
            rows.append(turn - np.floor(turn))
    return np.concatenate(rows).astype(np.float32)


def offset_columns():
    child, parent = offsets()
    return np.broadcast_to(np.concatenate([child, parent])[:, None], (3 * Q, LANES)).astype(np.float32)


def half_turn(phase):
    r = phase - jnp.round(phase)
    q = r * r
    s = SIN[3]
    for coefficient in SIN[2::-1]:
        s = s * q + coefficient
    s = s * r
    c = COS[3]
    for coefficient in COS[2::-1]:
        c = c * q + coefficient
    return 1.0 - s * s, s * c


def root(square):
    return square * lax.rsqrt(square)


def corner(own_boxes, box):
    position = lax.axis_index("grp") * lax.axis_size("dev") + lax.axis_index("dev")
    box_id = position * own_boxes + box
    return (box_id // ROW) * SIDE - GRID // 2, (box_id % ROW) * SIDE - GRID // 2


def outer(column, tile):
    return jnp.concatenate([column[j : j + 1] + tile for j in range(Q)], axis=0)


def source_box(own_boxes, targets, parents, b, weights_ref, table_ref, centre_ref, offset_ref, delta_ref):
    k1, k2 = corner(own_boxes, b)
    k1f, k2f = k1.astype(F32), k2.astype(F32)
    offs = offset_ref[...]
    for g in range(targets // LANES):
        lanes = slice(g * LANES, (g + 1) * LANES)
        lane = lax.broadcasted_iota(jnp.int32, (1, LANES), 1)
        box = lane + g * LANES
        h1 = 2 * WIDTH * (box // COLS) + WIDTH - 1
        h2 = 2 * WIDTH * (box % COLS) + WIDTH - 1
        whole = ((h1 * k1 + h2 * k2) & (2 * GRID - 1)).astype(F32) * (1.0 / (2 * GRID))
        c1 = centre_ref[0:1, lanes]
        c2 = centre_ref[1:2, lanes]
        first = c1 * (k1f + offs)
        first = first * first
        second = c2 * (k2f + offs)
        second = second * second
        turn1 = centre_ref[8 : 8 + 2 * Q, lanes]
        turn2 = centre_ref[8 + 2 * Q : 8 + 4 * Q, lanes] + whole
        back1 = centre_ref[8 + 4 * Q : 8 + 5 * Q, lanes]
        back2 = centre_ref[8 + 5 * Q : 8 + 6 * Q, lanes] + whole
        parent_lane = (g * (COLS // 2)) % LANES + (lane % COLS) // 2
        pick = jnp.broadcast_to(parent_lane, (R, LANES))
        start = (g * (COLS // 2)) // LANES * LANES
        high, low = [], []
        for u in range(2):
            for v in range(2):
                one, two = slice(u * Q, (u + 1) * Q), slice(v * Q, (v + 1) * Q)
                phase = root(outer(first[one], second[two])) + outer(turn1[one], turn2[two])
                cosine, sine = half_turn(phase)
                spread = []
                for z in range(2):
                    w = weights_ref[z, b, 2 * u + v, :, start : min(start + LANES, parents)]
                    if w.shape[1] < LANES:
                        w = jnp.concatenate([w] * (LANES // w.shape[1]), axis=1)
                    spread.append(jnp.take_along_axis(w, pick, axis=1, mode="promise_in_bounds"))
                wr, wi = spread
                both = jnp.concatenate([wr * cosine + wi * sine, wi * cosine - wr * sine], axis=1)
                top = both.astype(BF16)
                high.append(top)
                low.append((both - top.astype(F32)).astype(BF16))
        moved = jnp.concatenate(high + high + low, axis=0)
        interp = jnp.dot(table_ref[...], moved, preferred_element_type=F32)
        ir, ii = interp[:, :LANES], interp[:, LANES:]
        parent = slice(2 * Q, 3 * Q)
        phase = root(outer(first[parent], second[parent])) + outer(back1, back2)
        cosine, sine = half_turn(phase)
        for z, part in enumerate((ir * cosine - ii * sine, ii * cosine + ir * sine)):
            top = part.astype(BF16)
            delta_ref[b, z * R : (z + 1) * R, lanes] = top
            delta_ref[b, z * R : (z + 1) * R, targets + g * LANES : targets + (g + 1) * LANES] = (
                part - top.astype(F32)
            ).astype(BF16)


def skeleton_rows(own_boxes, targets, c, span, delta_ref, facts, firsts, ends, offs):
    row = lax.broadcasted_iota(jnp.int32, (span, targets), 0) + c * span
    hot = jnp.where((firsts <= row) & (row < ends), 1.0, 0.0).astype(BF16)
    contract = (((1,), (1,)), ((), ()))
    here = lax.dot_general(facts, hot, contract, preferred_element_type=F32).astype(jnp.int32)
    twice = jnp.concatenate([hot, hot], axis=1)
    place = lax.broadcasted_iota(jnp.int32, (1, span), 1) + c * span
    rank = place - (here[2 * RT + 2 : 2 * RT + 3] * LANES + here[2 * RT + 3 : 2 * RT + 4])
    mine = lax.broadcasted_iota(jnp.int32, (RT, span), 0) == rank
    p1 = jnp.sum(jnp.where(mine, here[:RT], 0), axis=0, keepdims=True)
    p2 = jnp.sum(jnp.where(mine, here[RT : 2 * RT], 0), axis=0, keepdims=True)
    h1 = here[2 * RT : 2 * RT + 1] * WIDTH + p1
    h2 = here[2 * RT + 1 : 2 * RT + 2] * WIDTH + p2
    x1 = h1.astype(F32) * (1.0 / GRID)
    x2 = h2.astype(F32) * (1.0 / GRID)
    angle = jnp.concatenate([h1, h2], axis=0)
    angle = ((8 * angle) & (GRID - 1)).astype(F32) * (2.0 * math.pi / GRID)
    sines, cosines = jnp.sin(angle), jnp.cos(angle)
    c1 = (2.0 + sines[0:1] * sines[1:2]) * (1.0 / 16)
    c2 = (2.0 + cosines[0:1] * cosines[1:2]) * (1.0 / 16)
    turn1 = x1 * offs
    turn1 = turn1 - jnp.floor(turn1)
    turn2 = x2 * offs
    turn2 = turn2 - jnp.floor(turn2)
    first = c1 * (corner(own_boxes, 0)[0].astype(F32) + offs)
    first = first * first
    sums = []
    for b in range(own_boxes):
        k1, k2 = corner(own_boxes, b)
        picked = lax.dot_general(delta_ref[b], twice, contract, preferred_element_type=F32)
        wr, wi = picked[:R], picked[R:]
        whole = ((h1 * k1 + h2 * k2) & (GRID - 1)).astype(F32) * (1.0 / GRID)
        second = c2 * (k2.astype(F32) + offs)
        second = second * second
        phase = root(outer(first, second)) + outer(turn1, turn2 + whole)
        cosine, sine = half_turn(phase)
        real = wr * cosine - wi * sine
        imag = wr * sine + wi * cosine
        sums.append((jnp.sum(real.reshape(Q, Q, span), axis=0), jnp.sum(imag.reshape(Q, Q, span), axis=0)))
    rows = [
        jnp.sum(sums[b][z] + sums[b + 1][z], axis=0, keepdims=True) for z in range(2) for b in range(0, own_boxes, 2)
    ]
    return jnp.concatenate(rows, axis=0)


def kernel(
    own_boxes, targets, parents, devices, depth,
    weights_hbm, pivots_ref, ranks_ref, owner_ref, table_hbm, centre_hbm, offset_ref, out_ref,
    weights, table, centre, all_pivots, delta, begin_row, begin, compact, rows,
    weights_sem, const_sem, begin_sem, pivot_send, pivot_recv, rows_send, rows_recv,
):
    me = lax.axis_index("grp") * depth + lax.axis_index("dev")

    def device(index):
        return (index // depth, index % depth)

    loads = [
        pltpu.make_async_copy(weights_hbm.at[:, b], weights.at[:, b], weights_sem.at[b]) for b in range(own_boxes)
    ]
    consts = [
        pltpu.make_async_copy(table_hbm, table, const_sem.at[0]),
        pltpu.make_async_copy(centre_hbm, centre, const_sem.at[1]),
    ]
    for copy in consts + loads:
        copy.start()
    barrier = pltpu.get_barrier_semaphore()

    def greet(j, carry):
        pl.semaphore_signal(
            barrier, inc=1, device_id=device(lax.rem(me + j, devices)), device_id_type=pl.DeviceIdType.MESH
        )
        return carry

    lax.fori_loop(1, devices, greet, 0)

    ranks = ranks_ref[...]
    owners = owner_ref[...]
    rank_down = jnp.broadcast_to(ranks, (targets, targets)).T
    owner_down = jnp.broadcast_to(owners, (targets, targets)).T
    slots = lax.broadcasted_iota(jnp.int32, (1, targets), 1)
    firsts = jnp.sum(jnp.where(owner_down < owners, rank_down, 0), axis=0, keepdims=True)
    ends = firsts + ranks
    begins = jnp.sum(jnp.where(owner_down < slots, rank_down, 0), axis=0, keepdims=True)
    begin_row[:, :targets] = begins
    begin_row[:, targets:] = jnp.full((1, LANES), targets * RMEAN, jnp.int32)
    to_scalars = pltpu.make_async_copy(begin_row, begin, begin_sem)
    to_scalars.start()

    pl.semaphore_wait(barrier, devices - 1)

    def pivot_copy(target, source):
        return pltpu.make_async_remote_copy(
            src_ref=pivots_ref,
            dst_ref=all_pivots.at[source],
            send_sem=pivot_send.at[target],
            recv_sem=pivot_recv.at[source],
            device_id=device(target),
            device_id_type=pl.DeviceIdType.MESH,
        )

    def send_pivots(j, carry):
        pivot_copy(lax.rem(me + j, devices), me).start()
        return carry

    lax.fori_loop(1, devices, send_pivots, 0)
    all_pivots[me] = pivots_ref[...]
    for copy in consts:
        copy.wait()

    def one_box(b, carry):
        pltpu.make_async_copy(weights_hbm.at[:, b], weights.at[:, b], weights_sem.at[b]).wait()
        source_box(own_boxes, targets, parents, b, weights, table, centre, offset_ref, delta)
        return carry

    lax.fori_loop(0, own_boxes, one_box, 0)

    def wait_pivots(j, carry):
        other = lax.rem(me + j, devices)
        copy = pivot_copy(other, other)
        copy.wait_send()
        copy.wait_recv()
        return carry

    lax.fori_loop(1, devices, wait_pivots, 0)
    columns = all_pivots[...].reshape(targets, RT).astype(F32).T.astype(jnp.int32)
    facts = jnp.concatenate(
        [columns // WIDTH, columns % WIDTH, slots // COLS, slots % COLS, firsts // LANES, firsts % LANES]
        + [jnp.zeros((12, targets), jnp.int32)],
        axis=0,
    )
    facts = facts.astype(F32).astype(BF16)
    offs = offset_ref[2 * Q : 3 * Q]
    span = 2 * LANES
    offs = jnp.concatenate([offs, offs], axis=1)
    chunks = targets * RMEAN // span

    def one_chunk(c, carry):
        block = skeleton_rows(own_boxes, targets, c, span, delta, facts, firsts, ends, offs)
        compact[2 * c] = block[:, :LANES]
        compact[2 * c + 1] = block[:, LANES:]
        return carry

    lax.fori_loop(0, chunks, one_chunk, 0)
    compact[2 * chunks] = jnp.zeros((own_boxes, LANES), F32)
    to_scalars.wait()
    boxes = LANES // RT
    groups = targets // devices // boxes
    lane = lax.broadcasted_iota(jnp.int32, (own_boxes, LANES), 1)

    def place_rows(owner, n):
        slot = (owner * groups + n) * boxes
        chunk = jnp.minimum(jnp.maximum(begin[0, slot], 0) // LANES, 2 * chunks - 1)
        low = jnp.full((own_boxes, LANES), begin[0, slot], jnp.int32)
        high = jnp.full((own_boxes, LANES), begin[0, slot + 1], jnp.int32)
        for k in range(1, boxes):
            low = jnp.where(lane >= k * RT, begin[0, slot + k], low)
            high = jnp.where(lane >= k * RT, begin[0, slot + k + 1], high)
        index = low + (lane & (RT - 1))
        local = index - chunk * LANES
        within = local & (LANES - 1)
        near = jnp.take_along_axis(compact[chunk], within, axis=1, mode="promise_in_bounds")
        far = jnp.take_along_axis(compact[chunk + 1], within, axis=1, mode="promise_in_bounds")
        return jnp.where(index < high, jnp.where(local >= LANES, far, near), 0.0)

    def rows_copy(target, source):
        return pltpu.make_async_remote_copy(
            src_ref=rows.at[target],
            dst_ref=out_ref.at[source],
            send_sem=rows_send.at[target],
            recv_sem=rows_recv.at[source],
            device_id=device(target),
            device_id_type=pl.DeviceIdType.MESH,
        )

    def send_rows(j, carry):
        other = lax.rem(me + j, devices)
        for n in range(groups):
            rows[other, n] = place_rows(other, n)
        rows_copy(other, me).start()
        return carry

    lax.fori_loop(1, devices, send_rows, 0)
    for n in range(groups):
        out_ref[me, n] = place_rows(me, n)

    def wait_rows(j, carry):
        other = lax.rem(me + j, devices)
        copy = rows_copy(other, other)
        copy.wait_send()
        copy.wait_recv()
        return carry

    lax.fori_loop(1, devices, wait_rows, 0)


def local(child_weights, pivots, ranks, owner_slot):
    depth = lax.axis_size("dev")
    devices = lax.axis_size("grp") * depth
    own_boxes = child_weights.shape[1]
    parents = child_weights.shape[4]
    targets = ranks.shape[0]
    groups = targets // devices * RT // LANES
    chunks = targets * RMEAN // LANES
    vmem = pl.BlockSpec(memory_space=pltpu.VMEM)
    anywhere = pl.BlockSpec(memory_space=pl.ANY)
    table, centre, offs = split_table(), centre_rows(targets), offset_columns()
    dma = pltpu.SemaphoreType.DMA
    received = pl.pallas_call(
        lambda *refs: kernel(own_boxes, targets, parents, devices, depth, *refs),
        in_specs=[anywhere, vmem, vmem, vmem, anywhere, anywhere, vmem],
        out_specs=vmem,
        out_shape=jax.ShapeDtypeStruct((devices, groups, own_boxes, LANES), F32),
        scratch_shapes=[
            pltpu.VMEM(child_weights.shape, F32),
            pltpu.VMEM(table.shape, BF16),
            pltpu.VMEM(centre.shape, F32),
            pltpu.VMEM((devices,) + pivots.shape, jnp.int32),
            pltpu.VMEM((own_boxes, 2 * R, 2 * targets), BF16),
            pltpu.VMEM((1, targets + LANES), jnp.int32),
            pltpu.SMEM((1, targets + LANES), jnp.int32),
            pltpu.VMEM((chunks + 1, own_boxes, LANES), F32),
            pltpu.VMEM((devices, groups, own_boxes, LANES), F32),
            dma((own_boxes,)),
            dma((2,)),
            dma,
            dma((devices,)),
            dma((devices,)),
            dma((devices,)),
            dma((devices,)),
        ],
        compiler_params=pltpu.CompilerParams(
            collective_id=0, has_side_effects=True, vmem_limit_bytes=48 << 20
        ),
    )(child_weights, pivots, ranks.reshape(1, targets), owner_slot.reshape(1, targets), table, centre, offs)

    halves = own_boxes // 2
    pair = ROW // own_boxes
    received = received.reshape(devices // (2 * pair), 2, pair, groups, 2, halves, LANES // RT, RT)
    summed = received[:, 0] + received[:, 1]
    result = jnp.transpose(summed, (3, 6, 2, 5, 0, 1, 4))
    return result.reshape(2, RT, targets // devices, devices * own_boxes // 4)


def solution(mesh):
    in_specs = (P(None, ("grp", "dev"), None, None, None), P(("grp", "dev"), None), P(), P())
    out_specs = P(None, None, ("grp", "dev"), None)
    return jax.shard_map(local, mesh=mesh, in_specs=in_specs, out_specs=out_specs, check_vma=False)
```

```python
import math

import jax
import jax.numpy as jnp
import numpy as np
from jax import lax
from jax.experimental import pallas as pl
from jax.experimental.pallas import tpu as pltpu
from jax.sharding import PartitionSpec as P

GRID = 2048
Q = 8
RT = 32
RMEAN = 10
SIDE = GRID // 32
WIDTH = GRID // 64
ROW = GRID // 64
COLS = GRID // 32
LANES = 128
R = Q * Q

SIN = (4.442867904603554, -7.30744348201647, 3.594788644821573, -0.7843755040132807)
COS = (1.414204082132758, -6.977642209183305, 5.715240371096478, -1.7283548501332477)

F32 = jnp.float32
BF16 = jnp.bfloat16
CONTRACT = (((1,), (1,)), ((), ()))


def nodes():
    return np.cos(np.pi * (2.0 * np.arange(Q) + 1.0) / (2.0 * Q))


def lagrange(at, points):
    out = np.ones((Q, Q))
    for t in range(Q):
        for k in range(Q):
            if k != t:
                out[t] *= (points - at[k]) / (at[t] - at[k])
    return out


def child_table():
    c = nodes()
    halves = np.stack([lagrange(c, u - 0.5 + 0.5 * c) for u in (0.0, 1.0)])
    return np.einsum("uaj,vbk->abuvjk", halves, halves).reshape(R, 4 * R)


def split_table():
    table = child_table().astype(np.float32)
    high = table.astype(jnp.bfloat16)
    low = (table - high.astype(np.float32)).astype(jnp.bfloat16)
    return np.concatenate([high, low, high], axis=1)


def offsets():
    c = nodes()
    parent = SIDE / 2 - 0.5 + SIDE / 2 * c
    child = np.concatenate([SIDE * u / 2 + SIDE / 4 - 0.5 + SIDE / 4 * c for u in (0, 1)])
    return child, parent


def centre_rows(targets):
    a = np.arange(targets)
    x1 = (2 * WIDTH * (a // COLS) + WIDTH - 1) / (2 * GRID)
    x2 = (2 * WIDTH * (a % COLS) + WIDTH - 1) / (2 * GRID)
    c1 = (2 + np.sin(16 * np.pi * x1) * np.sin(16 * np.pi * x2)) / 16
    c2 = (2 + np.cos(16 * np.pi * x1) * np.cos(16 * np.pi * x2)) / 16
    child, parent = offsets()
    rows = [np.stack([c1, c2] + [np.zeros(targets)] * 6)]
    for o in (child, parent):
        for x in (x1, x2):
            turn = o[:, None] * x[None, :]
            rows.append(turn - np.floor(turn))
    return np.concatenate(rows).astype(np.float32)


def offset_columns():
    child, parent = offsets()
    return np.broadcast_to(np.concatenate([child, parent])[:, None], (3 * Q, LANES)).astype(np.float32)


def half_turn(phase):
    r = phase - jnp.round(phase)
    q = r * r
    s = SIN[3]
    for coefficient in SIN[2::-1]:
        s = s * q + coefficient
    s = s * r
    c = COS[3]
    for coefficient in COS[2::-1]:
        c = c * q + coefficient
    return 1.0 - s * s, s * c


def root(square):
    return square * lax.rsqrt(square)


def corner(own_boxes, box):
    position = lax.axis_index("grp") * lax.axis_size("dev") + lax.axis_index("dev")
    box_id = position * own_boxes + box
    return (box_id // ROW) * SIDE - GRID // 2, (box_id % ROW) * SIDE - GRID // 2


def outer(column, tile):
    return jnp.concatenate([column[j : j + 1] + tile for j in range(Q)], axis=0)


def source_box(own_boxes, targets, parents, b, weights_ref, table_ref, centre_ref, offset_ref, delta_ref):
    k1, k2 = corner(own_boxes, b)
    k1f, k2f = k1.astype(F32), k2.astype(F32)
    offs = offset_ref[...]
    for g in range(targets // LANES):
        lanes = slice(g * LANES, (g + 1) * LANES)
        lane = lax.broadcasted_iota(jnp.int32, (1, LANES), 1)
        box = lane + g * LANES
        h1 = 2 * WIDTH * (box // COLS) + WIDTH - 1
        h2 = 2 * WIDTH * (box % COLS) + WIDTH - 1
        whole = ((h1 * k1 + h2 * k2) & (2 * GRID - 1)).astype(F32) * (1.0 / (2 * GRID))
        c1 = centre_ref[0:1, lanes]
        c2 = centre_ref[1:2, lanes]
        first = c1 * (k1f + offs)
        first = first * first
        second = c2 * (k2f + offs)
        second = second * second
        turn1 = centre_ref[8 : 8 + 2 * Q, lanes]
        turn2 = centre_ref[8 + 2 * Q : 8 + 4 * Q, lanes] + whole
        back1 = centre_ref[8 + 4 * Q : 8 + 5 * Q, lanes]
        back2 = centre_ref[8 + 5 * Q : 8 + 6 * Q, lanes] + whole
        parent_lane = (g * (COLS // 2)) % LANES + (lane % COLS) // 2
        pick = jnp.broadcast_to(parent_lane, (R, LANES))
        start = (g * (COLS // 2)) // LANES * LANES
        high, low = [], []
        for u in range(2):
            for v in range(2):
                one, two = slice(u * Q, (u + 1) * Q), slice(v * Q, (v + 1) * Q)
                phase = root(outer(first[one], second[two])) + outer(turn1[one], turn2[two])
                cosine, sine = half_turn(phase)
                spread = []
                for z in range(2):
                    w = weights_ref[z, b, 2 * u + v, :, start : min(start + LANES, parents)]
                    if w.shape[1] < LANES:
                        w = jnp.concatenate([w] * (LANES // w.shape[1]), axis=1)
                    spread.append(jnp.take_along_axis(w, pick, axis=1, mode="promise_in_bounds"))
                wr, wi = spread
                both = jnp.concatenate([wr * cosine + wi * sine, wi * cosine - wr * sine], axis=1)
                top = both.astype(BF16)
                high.append(top)
                low.append((both - top.astype(F32)).astype(BF16))
        moved = jnp.concatenate(high + high + low, axis=0)
        interp = jnp.dot(table_ref[...], moved, preferred_element_type=F32)
        ir, ii = interp[:, :LANES], interp[:, LANES:]
        parent = slice(2 * Q, 3 * Q)
        phase = root(outer(first[parent], second[parent])) + outer(back1, back2)
        cosine, sine = half_turn(phase)
        for z, part in enumerate((ir * cosine - ii * sine, ii * cosine + ir * sine)):
            top = part.astype(BF16)
            delta_ref[b, z * R : (z + 1) * R, lanes] = top
            delta_ref[b, z * R : (z + 1) * R, targets + g * LANES : targets + (g + 1) * LANES] = (
                part - top.astype(F32)
            ).astype(BF16)


def row_facts(targets, c, span, facts, firsts, ends):
    row = lax.broadcasted_iota(jnp.int32, (span, targets), 0) + c * span
    hot = jnp.where((firsts <= row) & (row < ends), 1.0, 0.0).astype(BF16)
    here = lax.dot_general(facts, hot, CONTRACT, preferred_element_type=F32).astype(jnp.int32)
    place = lax.broadcasted_iota(jnp.int32, (1, span), 1) + c * span
    rank = place - (here[2 * RT + 2 : 2 * RT + 3] * LANES + here[2 * RT + 3 : 2 * RT + 4])
    mine = lax.broadcasted_iota(jnp.int32, (RT, span), 0) == rank
    p1 = jnp.sum(jnp.where(mine, here[:RT], 0), axis=0, keepdims=True)
    p2 = jnp.sum(jnp.where(mine, here[RT : 2 * RT], 0), axis=0, keepdims=True)
    h1 = here[2 * RT : 2 * RT + 1] * WIDTH + p1
    h2 = here[2 * RT + 1 : 2 * RT + 2] * WIDTH + p2
    points = jnp.concatenate([h1, h2], axis=0)
    angle = ((8 * points) & (GRID - 1)).astype(F32) * (2.0 * math.pi / GRID)
    sines, cosines = jnp.sin(angle), jnp.cos(angle)
    c1 = (2.0 + sines[0:1] * sines[1:2]) * (1.0 / 16)
    c2 = (2.0 + cosines[0:1] * cosines[1:2]) * (1.0 / 16)
    return hot, jnp.concatenate([points.astype(F32), c1, c2], axis=0)


def skeleton_rows(own_boxes, boxes, span, hot, point, delta_ref, offs):
    twice = jnp.concatenate([hot, hot], axis=1)
    h1, h2 = point[0:1].astype(jnp.int32), point[1:2].astype(jnp.int32)
    c1, c2 = point[2:3], point[3:4]
    turn1 = point[0:1] * (1.0 / GRID) * offs
    turn1 = turn1 - jnp.floor(turn1)
    turn2 = point[1:2] * (1.0 / GRID) * offs
    turn2 = turn2 - jnp.floor(turn2)
    first = c1 * (corner(own_boxes, 0)[0].astype(F32) + offs)
    first = first * first
    sums = []
    for b in boxes:
        k1, k2 = corner(own_boxes, b)
        picked = lax.dot_general(delta_ref[b], twice, CONTRACT, preferred_element_type=F32)
        wr, wi = picked[:R], picked[R:]
        whole = ((h1 * k1 + h2 * k2) & (GRID - 1)).astype(F32) * (1.0 / GRID)
        second = c2 * (k2.astype(F32) + offs)
        second = second * second
        phase = root(outer(first, second)) + outer(turn1, turn2 + whole)
        cosine, sine = half_turn(phase)
        real = wr * cosine - wi * sine
        imag = wr * sine + wi * cosine
        sums.append((jnp.sum(real.reshape(Q, Q, span), axis=0), jnp.sum(imag.reshape(Q, Q, span), axis=0)))
    return jnp.concatenate(
        [
            jnp.sum(sums[n][z] + sums[n + 1][z], axis=0, keepdims=True)
            for z in range(2)
            for n in range(0, len(boxes), 2)
        ],
        axis=0,
    )


def kernel(
    own_boxes, targets, parents, devices, depth,
    weights_hbm, pivots_hbm, ranks_hbm, owner_hbm, table_hbm, centre_hbm, offset_hbm, out_ref,
    weights, table, centre, offset, ranks_row, owner_row, all_pivots, delta, begin_row, begin,
    hots, points, compact, places, rows,
    weights_sem, const_sem, begin_sem, pivot_send, pivot_recv, rows_send, rows_recv,
):
    me = lax.axis_index("grp") * depth + lax.axis_index("dev")
    span = 2 * LANES
    spans = targets * RMEAN // span

    def device(index):
        return (index // depth, index % depth)

    barrier = pltpu.get_barrier_semaphore()

    def greet(j, carry):
        pl.semaphore_signal(
            barrier, inc=1, device_id=device(lax.rem(me + j, devices)), device_id_type=pl.DeviceIdType.MESH
        )
        return carry

    pairs = [
        (ranks_hbm, ranks_row),
        (owner_hbm, owner_row),
        (table_hbm, table),
        (centre_hbm, centre),
        (offset_hbm, offset),
        (pivots_hbm, all_pivots.at[me]),
    ]
    consts = [pltpu.make_async_copy(far, near, const_sem.at[n]) for n, (far, near) in enumerate(pairs)]
    loads = [
        pltpu.make_async_copy(weights_hbm.at[:, b], weights.at[:, b], weights_sem.at[b]) for b in range(own_boxes)
    ]
    for copy in consts + loads:
        copy.start()
    lax.fori_loop(1, devices, greet, 0)
    for copy in consts:
        copy.wait()

    ranks = ranks_row[...]
    owners = owner_row[...]
    rank_down = jnp.broadcast_to(ranks, (targets, targets)).T
    owner_down = jnp.broadcast_to(owners, (targets, targets)).T
    slots = lax.broadcasted_iota(jnp.int32, (1, targets), 1)
    firsts = jnp.sum(jnp.where(owner_down < owners, rank_down, 0), axis=0, keepdims=True)
    ends = firsts + ranks
    begins = jnp.sum(jnp.where(owner_down < slots, rank_down, 0), axis=0, keepdims=True)
    begin_row[:, :targets] = begins
    begin_row[:, targets:] = jnp.full((1, LANES), targets * RMEAN, jnp.int32)
    to_scalars = pltpu.make_async_copy(begin_row, begin, begin_sem)
    to_scalars.start()

    def pivot_copy(target, source):
        return pltpu.make_async_remote_copy(
            src_ref=pivots_hbm,
            dst_ref=all_pivots.at[source],
            send_sem=pivot_send.at[target],
            recv_sem=pivot_recv.at[source],
            device_id=device(target),
            device_id_type=pl.DeviceIdType.MESH,
        )

    def send_pivots(j, carry):
        pivot_copy(lax.rem(me + j, devices), me).start()
        return carry

    def one_box(b, carry):
        pltpu.make_async_copy(weights_hbm.at[:, b], weights.at[:, b], weights_sem.at[b]).wait()
        source_box(own_boxes, targets, parents, b, weights, table, centre, offset, delta)
        return carry

    lax.fori_loop(0, 2, one_box, 0)
    pl.semaphore_wait(barrier, devices - 1)
    lax.fori_loop(1, devices, send_pivots, 0)
    lax.fori_loop(2, own_boxes, one_box, 0)

    to_scalars.wait()
    boxes = LANES // RT
    groups = targets // devices // boxes
    tall = own_boxes // 2
    lane = lax.broadcasted_iota(jnp.int32, (tall, LANES), 1)

    def chunk_of(slot):
        return jnp.minimum(jnp.maximum(begin[0, slot], 0) // LANES, 2 * spans - 1)

    def one_place(owner, carry):
        parts = []
        for n in range(groups):
            slot = (owner * groups + n) * boxes
            edges = [begin[0, slot + k] for k in range(boxes + 1)]
            low = jnp.full((tall, LANES), edges[0], jnp.int32)
            high = jnp.full((tall, LANES), edges[1], jnp.int32)
            for k in range(1, boxes):
                low = jnp.where(lane >= k * RT, edges[k], low)
                high = jnp.where(lane >= k * RT, edges[k + 1], high)
            index = low + (lane & (RT - 1))
            parts.append(jnp.where(index < high, index - chunk_of(slot) * LANES, -1))
        places[owner] = jnp.concatenate(parts, axis=0)
        return carry

    lax.fori_loop(0, devices, one_place, 0)

    def wait_pivots(j, carry):
        other = lax.rem(me + j, devices)
        copy = pivot_copy(other, other)
        copy.wait_send()
        copy.wait_recv()
        return carry

    lax.fori_loop(1, devices, wait_pivots, 0)
    columns = all_pivots[...].reshape(targets, RT).astype(F32).T.astype(jnp.int32)
    facts = jnp.concatenate(
        [columns // WIDTH, columns % WIDTH, slots // COLS, slots % COLS, firsts // LANES, firsts % LANES]
        + [jnp.zeros((12, targets), jnp.int32)],
        axis=0,
    )
    facts = facts.astype(F32).astype(BF16)
    offs = offset[2 * Q : 3 * Q]
    offs = jnp.concatenate([offs, offs], axis=1)

    def one_fact(c, carry):
        hot, point = row_facts(targets, c, span, facts, firsts, ends)
        hots[c] = hot
        points[c, 0:4] = point
        return carry

    lax.fori_loop(0, spans, one_fact, 0)
    compact[2 * spans] = jnp.zeros((tall * groups, LANES), F32)

    def rows_copy(half, target, source):
        return pltpu.make_async_remote_copy(
            src_ref=rows.at[half, target],
            dst_ref=out_ref.at[half, source],
            send_sem=rows_send.at[half, target],
            recv_sem=rows_recv.at[half, source],
            device_id=device(target),
            device_id_type=pl.DeviceIdType.MESH,
        )

    for half in range(2):
        mine = range(half * own_boxes // 2, (half + 1) * own_boxes // 2)

        def one_span(c, carry):
            block = skeleton_rows(own_boxes, mine, span, hots[c], points[c], delta, offs)
            block = jnp.concatenate([block] * groups, axis=0)
            compact[2 * c] = block[:, :LANES]
            compact[2 * c + 1] = block[:, LANES:]
            return carry

        def place_rows(owner):
            chunks = [chunk_of((owner * groups + n) * boxes) for n in range(groups)]
            near = jnp.concatenate(
                [compact[chunk][n * tall : (n + 1) * tall] for n, chunk in enumerate(chunks)], axis=0
            )
            far = jnp.concatenate(
                [compact[chunk + 1][n * tall : (n + 1) * tall] for n, chunk in enumerate(chunks)], axis=0
            )
            place = places[owner]
            within = place & (LANES - 1)
            near = jnp.take_along_axis(near, within, axis=1, mode="promise_in_bounds")
            far = jnp.take_along_axis(far, within, axis=1, mode="promise_in_bounds")
            return jnp.where(place < 0, 0.0, jnp.where(place >= LANES, far, near))

        def send_rows(j, carry):
            other = lax.rem(me + j, devices)
            rows[half, other] = place_rows(other)
            rows_copy(half, other, me).start()
            return carry

        lax.fori_loop(0, spans, one_span, 0)
        lax.fori_loop(1, devices, send_rows, 0)
        out_ref[half, me] = place_rows(me)

    def wait_rows(j, carry):
        other = lax.rem(me + j, devices)
        for half in range(2):
            copy = rows_copy(half, other, other)
            copy.wait_send()
            copy.wait_recv()
        return carry

    lax.fori_loop(1, devices, wait_rows, 0)


def local(child_weights, pivots, ranks, owner_slot):
    depth = lax.axis_size("dev")
    devices = lax.axis_size("grp") * depth
    own_boxes = child_weights.shape[1]
    parents = child_weights.shape[4]
    targets = ranks.shape[0]
    groups = targets // devices * RT // LANES
    tall = own_boxes // 2 * groups
    spans = targets * RMEAN // (2 * LANES)
    anywhere = pl.BlockSpec(memory_space=pl.ANY)
    table, centre, offs = split_table(), centre_rows(targets), offset_columns()
    dma = pltpu.SemaphoreType.DMA
    received = pl.pallas_call(
        lambda *refs: kernel(own_boxes, targets, parents, devices, depth, *refs),
        in_specs=[anywhere] * 7,
        out_specs=pl.BlockSpec(memory_space=pltpu.VMEM),
        out_shape=jax.ShapeDtypeStruct((2, devices, tall, LANES), F32),
        scratch_shapes=[
            pltpu.VMEM(child_weights.shape, F32),
            pltpu.VMEM(table.shape, BF16),
            pltpu.VMEM(centre.shape, F32),
            pltpu.VMEM(offs.shape, F32),
            pltpu.VMEM((1, targets), jnp.int32),
            pltpu.VMEM((1, targets), jnp.int32),
            pltpu.VMEM((devices,) + pivots.shape, jnp.int32),
            pltpu.VMEM((own_boxes, 2 * R, 2 * targets), BF16),
            pltpu.VMEM((1, targets + LANES), jnp.int32),
            pltpu.SMEM((1, targets + LANES), jnp.int32),
            pltpu.VMEM((spans, 2 * LANES, targets), BF16),
            pltpu.VMEM((spans, 8, 2 * LANES), F32),
            pltpu.VMEM((2 * spans + 1, tall, LANES), F32),
            pltpu.VMEM((devices, tall, LANES), jnp.int32),
            pltpu.VMEM((2, devices, tall, LANES), F32),
            dma((own_boxes,)),
            dma((6,)),
            dma,
            dma((devices,)),
            dma((devices,)),
            dma((2, devices)),
            dma((2, devices)),
        ],
        compiler_params=pltpu.CompilerParams(
            collective_id=0, has_side_effects=True, vmem_limit_bytes=60 << 20
        ),
    )(child_weights, pivots, ranks.reshape(1, targets), owner_slot.reshape(1, targets), table, centre, offs)

    quarter = own_boxes // 4
    pair = ROW // own_boxes
    received = received.reshape(2, devices // (2 * pair), 2, pair, groups, 2, quarter, LANES // RT, RT)
    summed = received[:, :, 0] + received[:, :, 1]
    result = jnp.transpose(summed, (4, 7, 3, 6, 1, 2, 0, 5))
    return result.reshape(2, RT, targets // devices, devices * own_boxes // 4)


def solution(mesh):
    in_specs = (P(None, ("grp", "dev"), None, None, None), P(("grp", "dev"), None), P(), P())
    out_specs = P(None, None, ("grp", "dev"), None)
    return jax.shard_map(local, mesh=mesh, in_specs=in_specs, out_specs=out_specs, check_vma=False)
```

```python
import math

import jax
import jax.numpy as jnp
import numpy as np
from jax import lax
from jax.experimental import pallas as pl
from jax.experimental.pallas import tpu as pltpu
from jax.sharding import PartitionSpec as P

GRID = 2048
Q = 8
RT = 32
RMEAN = 10
SIDE = GRID // 32
WIDTH = GRID // 64
ROW = GRID // 64
COLS = GRID // 32
LANES = 128
R = Q * Q

SIN = (4.442867904603554, -7.30744348201647, 3.594788644821573, -0.7843755040132807)
COS = (1.414204082132758, -6.977642209183305, 5.715240371096478, -1.7283548501332477)
FINE_SIN = (4.442882938082702, -7.308249478180419, 3.6064755519164122, -0.8474705853915653, 0.1160367907993074, -0.009939639006380334)
FINE_COS = (1.4142135623720344, -6.97886419922267, 5.739885708281956, -1.8883460761614363, 0.3328004285822709, -0.03645323263485946, 0.002602159860467781)

F32 = jnp.float32
BF16 = jnp.bfloat16
CONTRACT = (((1,), (1,)), ((), ()))


def nodes():
    return np.cos(np.pi * (2.0 * np.arange(Q) + 1.0) / (2.0 * Q))


def lagrange(at, points):
    out = np.ones((Q, Q))
    for t in range(Q):
        for k in range(Q):
            if k != t:
                out[t] *= (points - at[k]) / (at[t] - at[k])
    return out


def child_table():
    c = nodes()
    halves = np.stack([lagrange(c, u - 0.5 + 0.5 * c) for u in (0.0, 1.0)])
    return np.einsum("uaj,vbk->abuvjk", halves, halves).reshape(R, 4 * R)


def split_table():
    table = child_table().astype(np.float32)
    high = table.astype(jnp.bfloat16)
    low = (table - high.astype(np.float32)).astype(jnp.bfloat16)
    return np.concatenate([high, low, high], axis=1)


def offsets():
    c = nodes()
    parent = SIDE / 2 - 0.5 + SIDE / 2 * c
    child = np.concatenate([SIDE * u / 2 + SIDE / 4 - 0.5 + SIDE / 4 * c for u in (0, 1)])
    return child, parent


def centre_rows(targets):
    a = np.arange(targets)
    x1 = (2 * WIDTH * (a // COLS) + WIDTH - 1) / (2 * GRID)
    x2 = (2 * WIDTH * (a % COLS) + WIDTH - 1) / (2 * GRID)
    c1 = (2 + np.sin(16 * np.pi * x1) * np.sin(16 * np.pi * x2)) / 16
    c2 = (2 + np.cos(16 * np.pi * x1) * np.cos(16 * np.pi * x2)) / 16
    child, parent = offsets()
    rows = [np.stack([c1, c2] + [np.zeros(targets)] * 6)]
    for o in (child, parent):
        for x in (x1, x2):
            turn = o[:, None] * x[None, :]
            rows.append(turn - np.floor(turn))
    return np.concatenate(rows).astype(np.float32)


def offset_columns():
    child, parent = offsets()
    return np.broadcast_to(np.concatenate([child, parent])[:, None], (3 * Q, LANES)).astype(np.float32)


def half_turn(phase):
    r = phase - jnp.round(phase)
    q = r * r
    s = SIN[3]
    for coefficient in SIN[2::-1]:
        s = s * q + coefficient
    s = s * r
    c = COS[3]
    for coefficient in COS[2::-1]:
        c = c * q + coefficient
    return 1.0 - s * s, s * c


def exact_turn(r):
    q = r * r
    s, c = FINE_SIN[-1], FINE_COS[-1]
    for coefficient in FINE_SIN[-2::-1]:
        s = s * q + coefficient
    for coefficient in FINE_COS[-2::-1]:
        c = c * q + coefficient
    s = s * r
    return jnp.where(s * s < 1.0, 1.0 - s * s, c * c - 1.0), s * c


def root(square):
    return square * lax.rsqrt(square)


def corner(own_boxes, box):
    position = lax.axis_index("grp") * lax.axis_size("dev") + lax.axis_index("dev")
    box_id = position * own_boxes + box
    return (box_id // ROW) * SIDE - GRID // 2, (box_id % ROW) * SIDE - GRID // 2


def outer(column, tile):
    return jnp.concatenate([column[j : j + 1] + tile for j in range(Q)], axis=0)


def source_box(own_boxes, targets, parents, b, weights_ref, table_ref, centre_ref, offset_ref, delta_ref):
    k1, k2 = corner(own_boxes, b)
    k1f, k2f = k1.astype(F32), k2.astype(F32)
    offs = offset_ref[...]
    for g in range(targets // LANES):
        lanes = slice(g * LANES, (g + 1) * LANES)
        lane = lax.broadcasted_iota(jnp.int32, (1, LANES), 1)
        box = lane + g * LANES
        h1 = 2 * WIDTH * (box // COLS) + WIDTH - 1
        h2 = 2 * WIDTH * (box % COLS) + WIDTH - 1
        whole = ((h1 * k1 + h2 * k2) & (2 * GRID - 1)).astype(F32) * (1.0 / (2 * GRID))
        c1 = centre_ref[0:1, lanes]
        c2 = centre_ref[1:2, lanes]
        first = c1 * (k1f + offs)
        first = first * first
        second = c2 * (k2f + offs)
        second = second * second
        turn1 = centre_ref[8 : 8 + 2 * Q, lanes]
        turn2 = centre_ref[8 + 2 * Q : 8 + 4 * Q, lanes] + whole
        back1 = centre_ref[8 + 4 * Q : 8 + 5 * Q, lanes]
        back2 = centre_ref[8 + 5 * Q : 8 + 6 * Q, lanes] + whole
        parent_lane = (g * (COLS // 2)) % LANES + (lane % COLS) // 2
        pick = jnp.broadcast_to(parent_lane, (R, LANES))
        start = (g * (COLS // 2)) // LANES * LANES
        high, low = [], []
        for u in range(2):
            for v in range(2):
                one, two = slice(u * Q, (u + 1) * Q), slice(v * Q, (v + 1) * Q)
                phase = root(outer(first[one], second[two])) + outer(turn1[one], turn2[two])
                cosine, sine = half_turn(phase)
                spread = []
                for z in range(2):
                    w = weights_ref[z, b, 2 * u + v, :, start : min(start + LANES, parents)]
                    if w.shape[1] < LANES:
                        w = jnp.concatenate([w] * (LANES // w.shape[1]), axis=1)
                    spread.append(jnp.take_along_axis(w, pick, axis=1, mode="promise_in_bounds"))
                wr, wi = spread
                both = jnp.concatenate([wr * cosine + wi * sine, wi * cosine - wr * sine], axis=1)
                top = both.astype(BF16)
                high.append(top)
                low.append((both - top.astype(F32)).astype(BF16))
        moved = jnp.concatenate(high + high + low, axis=0)
        interp = jnp.dot(table_ref[...], moved, preferred_element_type=F32)
        ir, ii = interp[:, :LANES], interp[:, LANES:]
        parent = slice(2 * Q, 3 * Q)
        phase = root(outer(first[parent], second[parent])) + outer(back1, back2)
        cosine, sine = half_turn(phase)
        for z, part in enumerate((ir * cosine - ii * sine, ii * cosine + ir * sine)):
            top = part.astype(BF16)
            delta_ref[b, z * R : (z + 1) * R, lanes] = top
            delta_ref[b, z * R : (z + 1) * R, targets + g * LANES : targets + (g + 1) * LANES] = (
                part - top.astype(F32)
            ).astype(BF16)


def row_facts(targets, c, span, facts, firsts, ends):
    row = lax.broadcasted_iota(jnp.int32, (span, targets), 0) + c * span
    hot = jnp.where((firsts <= row) & (row < ends), 1.0, 0.0).astype(BF16)
    here = lax.dot_general(facts, hot, CONTRACT, preferred_element_type=F32).astype(jnp.int32)
    place = lax.broadcasted_iota(jnp.int32, (1, span), 1) + c * span
    rank = place - (here[2 * RT + 2 : 2 * RT + 3] * LANES + here[2 * RT + 3 : 2 * RT + 4])
    mine = lax.broadcasted_iota(jnp.int32, (RT, span), 0) == rank
    p1 = jnp.sum(jnp.where(mine, here[:RT], 0), axis=0, keepdims=True)
    p2 = jnp.sum(jnp.where(mine, here[RT : 2 * RT], 0), axis=0, keepdims=True)
    h1 = here[2 * RT : 2 * RT + 1] * WIDTH + p1
    h2 = here[2 * RT + 1 : 2 * RT + 2] * WIDTH + p2
    points = jnp.concatenate([h1, h2], axis=0)
    angle = ((8 * points) & (GRID - 1)).astype(F32) * (1.0 / GRID)
    cosines, sines = exact_turn(angle - jnp.where(angle > 0.5, 1.0, 0.0))
    c1 = (2.0 + sines[0:1] * sines[1:2]) * (1.0 / 16)
    c2 = (2.0 + cosines[0:1] * cosines[1:2]) * (1.0 / 16)
    return hot, jnp.concatenate([points.astype(F32), c1, c2], axis=0)


def skeleton_rows(own_boxes, boxes, span, hot, point, delta_ref, offs):
    twice = jnp.concatenate([hot, hot], axis=1)
    h1, h2 = point[0:1].astype(jnp.int32), point[1:2].astype(jnp.int32)
    c1, c2 = point[2:3], point[3:4]
    turn1 = point[0:1] * (1.0 / GRID) * offs
    turn1 = turn1 - jnp.floor(turn1)
    turn2 = point[1:2] * (1.0 / GRID) * offs
    turn2 = turn2 - jnp.floor(turn2)
    first = c1 * (corner(own_boxes, 0)[0].astype(F32) + offs)
    first = first * first
    sums = []
    for b in boxes:
        k1, k2 = corner(own_boxes, b)
        picked = lax.dot_general(delta_ref[b], twice, CONTRACT, preferred_element_type=F32)
        wr, wi = picked[:R], picked[R:]
        whole = ((h1 * k1 + h2 * k2) & (GRID - 1)).astype(F32) * (1.0 / GRID)
        second = c2 * (k2.astype(F32) + offs)
        second = second * second
        phase = root(outer(first, second)) + outer(turn1, turn2 + whole)
        cosine, sine = half_turn(phase)
        real = wr * cosine - wi * sine
        imag = wr * sine + wi * cosine
        sums.append((jnp.sum(real.reshape(Q, Q, span), axis=0), jnp.sum(imag.reshape(Q, Q, span), axis=0)))
    return jnp.concatenate(
        [
            jnp.sum(sums[n][z] + sums[n + 1][z], axis=0, keepdims=True)
            for z in range(2)
            for n in range(0, len(boxes), 2)
        ],
        axis=0,
    )


def kernel(
    own_boxes, targets, parents, devices, depth,
    weights_hbm, pivots_hbm, ranks_hbm, owner_hbm, table_hbm, centre_hbm, offset_hbm, out_ref,
    weights, table, centre, offset, ranks_row, owner_row, all_pivots, delta, begin_row, stop_row, chunk_row, chunks,
    hots, points, compact, places, rows,
    weights_sem, const_sem, begin_sem, pivot_send, pivot_recv, rows_send, rows_recv,
):
    me = lax.axis_index("grp") * depth + lax.axis_index("dev")
    span = 2 * LANES
    spans = targets * RMEAN // span

    def device(index):
        return (lax.div(index, depth), lax.rem(index, depth))

    barrier = pltpu.get_barrier_semaphore()

    def greet(j, carry):
        pl.semaphore_signal(
            barrier, inc=1, device_id=device(lax.rem(me + j, devices)), device_id_type=pl.DeviceIdType.MESH
        )
        return carry

    pairs = [
        (ranks_hbm, ranks_row),
        (owner_hbm, owner_row),
        (table_hbm, table),
        (centre_hbm, centre),
        (offset_hbm, offset),
        (pivots_hbm, all_pivots.at[me]),
    ]
    consts = [pltpu.make_async_copy(far, near, const_sem.at[n]) for n, (far, near) in enumerate(pairs)]
    loads = [
        pltpu.make_async_copy(weights_hbm.at[:, b], weights.at[:, b], weights_sem.at[b]) for b in range(own_boxes)
    ]
    for copy in consts + loads:
        copy.start()
    lax.fori_loop(1, devices, greet, 0)
    for copy in consts:
        copy.wait()

    ranks = ranks_row[...]
    owners = owner_row[...]
    rank_down = jnp.broadcast_to(ranks, (targets, targets)).T
    owner_down = jnp.broadcast_to(owners, (targets, targets)).T
    slots = lax.broadcasted_iota(jnp.int32, (1, targets), 1)
    firsts = jnp.sum(jnp.where(owner_down < owners, rank_down, 0), axis=0, keepdims=True)
    ends = firsts + ranks
    begins = jnp.sum(jnp.where(owner_down < slots, rank_down, 0), axis=0, keepdims=True)
    begin_row[...] = begins
    stop_row[...] = jnp.sum(jnp.where(owner_down <= slots, rank_down, 0), axis=0, keepdims=True)
    chunk_row[...] = jnp.minimum(begins // LANES, 2 * spans - 1)
    to_scalars = pltpu.make_async_copy(chunk_row, chunks, begin_sem)
    to_scalars.start()

    def pivot_copy(target, source):
        return pltpu.make_async_remote_copy(
            src_ref=pivots_hbm,
            dst_ref=all_pivots.at[source],
            send_sem=pivot_send,
            recv_sem=pivot_recv,
            device_id=device(target),
            device_id_type=pl.DeviceIdType.MESH,
        )

    def send_pivots(j, carry):
        pivot_copy(lax.rem(me + j, devices), me).start()
        return carry

    def one_box(b, carry):
        pltpu.make_async_copy(weights_hbm.at[:, b], weights.at[:, b], weights_sem.at[b]).wait()
        source_box(own_boxes, targets, parents, b, weights, table, centre, offset, delta)
        return carry

    lax.fori_loop(0, 2, one_box, 0)
    pl.semaphore_wait(barrier, devices - 1)
    lax.fori_loop(1, devices, send_pivots, 0)
    lax.fori_loop(2, own_boxes, one_box, 0)

    boxes = LANES // RT
    groups = targets // devices // boxes
    tall = own_boxes // 2
    down = lax.broadcasted_iota(jnp.int32, (tall * groups, LANES), 0)
    lane = lax.broadcasted_iota(jnp.int32, (tall * groups, LANES), 1)
    opening = (down // tall) * boxes
    slot_here = opening + lane // RT
    per_tile = LANES // (groups * boxes)

    def one_tile(n, carry):
        for m in range(per_tile):
            spot = pl.ds(pl.multiple_of(n * LANES, LANES), LANES)
            first = jnp.broadcast_to(begin_row[:, spot], lane.shape)
            last = jnp.broadcast_to(stop_row[:, spot], lane.shape)
            tile_slot = slot_here + m * groups * boxes
            low = jnp.take_along_axis(first, tile_slot, axis=1, mode="promise_in_bounds")
            high = jnp.take_along_axis(last, tile_slot, axis=1, mode="promise_in_bounds")
            start = jnp.take_along_axis(first, opening + m * groups * boxes, axis=1, mode="promise_in_bounds")
            index = low + (lane & (RT - 1))
            places[n * per_tile + m] = jnp.where(index < high, index - (start & -LANES), -1)
        return carry

    lax.fori_loop(0, targets // LANES, one_tile, 0)
    to_scalars.wait()

    def drain(block, send, receive):
        copy = pltpu.make_async_remote_copy(
            src_ref=block,
            dst_ref=block,
            send_sem=send,
            recv_sem=receive,
            device_id=device(lax.rem(me + 1, devices)),
            device_id_type=pl.DeviceIdType.MESH,
        )
        copy.wait_send()
        copy.wait_recv()

    others = pl.ds(0, devices - 1)
    drain(all_pivots.at[others], pivot_send, pivot_recv)
    columns = all_pivots[...].reshape(targets, RT).astype(F32).T.astype(jnp.int32)
    facts = jnp.concatenate(
        [columns // WIDTH, columns % WIDTH, slots // COLS, slots % COLS, firsts // LANES, firsts % LANES]
        + [jnp.zeros((12, targets), jnp.int32)],
        axis=0,
    )
    facts = facts.astype(F32).astype(BF16)
    offs = offset[2 * Q : 3 * Q]
    offs = jnp.concatenate([offs, offs], axis=1)

    def one_fact(c, carry):
        hot, point = row_facts(targets, c, span, facts, firsts, ends)
        hots[c] = hot
        points[c, 0:4] = point
        return carry

    lax.fori_loop(0, spans, one_fact, 0, unroll=5 if spans % 5 == 0 else 1)
    compact[2 * spans] = jnp.zeros((tall * groups, LANES), F32)

    def rows_copy(half, target, source):
        return pltpu.make_async_remote_copy(
            src_ref=rows.at[half, target],
            dst_ref=out_ref.at[half, source],
            send_sem=rows_send,
            recv_sem=rows_recv,
            device_id=device(target),
            device_id_type=pl.DeviceIdType.MESH,
        )

    for half in range(2):
        mine = range(half * own_boxes // 2, (half + 1) * own_boxes // 2)

        def one_span(c, carry):
            block = skeleton_rows(own_boxes, mine, span, hots[c], points[c], delta, offs)
            block = jnp.concatenate([block] * groups, axis=0)
            compact[2 * c] = block[:, :LANES]
            compact[2 * c + 1] = block[:, LANES:]
            return carry

        def place_rows(owner, carry):
            slot = owner * groups * boxes
            near, far = compact[chunks[0, slot]], compact[chunks[0, slot] + 1]
            for n in range(1, groups):
                chunk = chunks[0, slot + n * boxes]
                near = jnp.where(down >= n * tall, compact[chunk], near)
                far = jnp.where(down >= n * tall, compact[chunk + 1], far)
            place = places[owner]
            within = place & (LANES - 1)
            near = jnp.take_along_axis(near, within, axis=1, mode="promise_in_bounds")
            far = jnp.take_along_axis(far, within, axis=1, mode="promise_in_bounds")
            rows[half, owner] = jnp.where(place < 0, 0.0, jnp.where(place >= LANES, far, near))
            return carry

        def send_rows(j, carry):
            rows_copy(half, lax.rem(me + j, devices), me).start()
            return carry

        lax.fori_loop(0, spans, one_span, 0)
        lax.fori_loop(0, devices, place_rows, 0, unroll=8)
        lax.fori_loop(1, devices, send_rows, 0)
        out_ref[half, me] = rows[half, me]

    drain(out_ref.at[:, others], rows_send, rows_recv)


def local(child_weights, pivots, ranks, owner_slot):
    depth = lax.axis_size("dev")
    devices = lax.axis_size("grp") * depth
    own_boxes = child_weights.shape[1]
    parents = child_weights.shape[4]
    targets = ranks.shape[0]
    groups = targets // devices * RT // LANES
    tall = own_boxes // 2 * groups
    spans = targets * RMEAN // (2 * LANES)
    anywhere = pl.BlockSpec(memory_space=pl.ANY)
    table, centre, offs = split_table(), centre_rows(targets), offset_columns()
    dma = pltpu.SemaphoreType.DMA
    received = pl.pallas_call(
        lambda *refs: kernel(own_boxes, targets, parents, devices, depth, *refs),
        in_specs=[anywhere] * 7,
        out_specs=pl.BlockSpec(memory_space=pltpu.VMEM),
        out_shape=jax.ShapeDtypeStruct((2, devices, tall, LANES), F32),
        scratch_shapes=[
            pltpu.VMEM(child_weights.shape, F32),
            pltpu.VMEM(table.shape, BF16),
            pltpu.VMEM(centre.shape, F32),
            pltpu.VMEM(offs.shape, F32),
            pltpu.VMEM((1, targets), jnp.int32),
            pltpu.VMEM((1, targets), jnp.int32),
            pltpu.VMEM((devices,) + pivots.shape, jnp.int32),
            pltpu.VMEM((own_boxes, 2 * R, 2 * targets), BF16),
            pltpu.VMEM((1, targets), jnp.int32),
            pltpu.VMEM((1, targets), jnp.int32),
            pltpu.VMEM((1, targets), jnp.int32),
            pltpu.SMEM((1, targets), jnp.int32),
            pltpu.VMEM((spans, 2 * LANES, targets), BF16),
            pltpu.VMEM((spans, 8, 2 * LANES), F32),
            pltpu.VMEM((2 * spans + 1, tall, LANES), F32),
            pltpu.VMEM((devices, tall, LANES), jnp.int32),
            pltpu.VMEM((2, devices, tall, LANES), F32),
            dma((own_boxes,)),
            dma((6,)),
            dma,
            dma,
            dma,
            dma,
            dma,
        ],
        compiler_params=pltpu.CompilerParams(
            collective_id=0, has_side_effects=True, vmem_limit_bytes=60 << 20
        ),
    )(child_weights, pivots, ranks.reshape(1, targets), owner_slot.reshape(1, targets), table, centre, offs)

    quarter = own_boxes // 4
    pair = ROW // own_boxes
    received = received.reshape(2, devices // (2 * pair), 2, pair, groups, 2, quarter, LANES // RT, RT)
    summed = received[:, :, 0] + received[:, :, 1]
    result = jnp.transpose(summed, (4, 7, 3, 6, 1, 2, 0, 5))
    return result.reshape(2, RT, targets // devices, devices * own_boxes // 4)


def solution(mesh):
    in_specs = (P(None, ("grp", "dev"), None, None, None), P(("grp", "dev"), None), P(), P())
    out_specs = P(None, None, ("grp", "dev"), None)
    return jax.shard_map(local, mesh=mesh, in_specs=in_specs, out_specs=out_specs, check_vma=False)
```

```python
import math

import jax
import jax.numpy as jnp
import numpy as np
from jax import lax
from jax.experimental import pallas as pl
from jax.experimental.pallas import tpu as pltpu
from jax.sharding import PartitionSpec as P

GRID = 2048
Q = 8
RT = 32
RMEAN = 10
SIDE = GRID // 32
WIDTH = GRID // 64
ROW = GRID // 64
COLS = GRID // 32
LANES = 128
WHOLE = 1.5 * 2**23
R = Q * Q

SIN = (4.442867904603554, -7.30744348201647, 3.594788644821573, -0.7843755040132807)
COS = (1.414204082132758, -6.977642209183305, 5.715240371096478, -1.7283548501332477)
FINE_SIN = (4.442882938082702, -7.308249478180419, 3.6064755519164122, -0.8474705853915653, 0.1160367907993074, -0.009939639006380334)
FINE_COS = (1.4142135623720344, -6.97886419922267, 5.739885708281956, -1.8883460761614363, 0.3328004285822709, -0.03645323263485946, 0.002602159860467781)

F32 = jnp.float32
BF16 = jnp.bfloat16
CONTRACT = (((1,), (1,)), ((), ()))


def nodes():
    return np.cos(np.pi * (2.0 * np.arange(Q) + 1.0) / (2.0 * Q))


def lagrange(at, points):
    out = np.ones((Q, Q))
    for t in range(Q):
        for k in range(Q):
            if k != t:
                out[t] *= (points - at[k]) / (at[t] - at[k])
    return out


def child_table():
    c = nodes()
    halves = np.stack([lagrange(c, u - 0.5 + 0.5 * c) for u in (0.0, 1.0)])
    return np.einsum("uaj,vbk->abuvjk", halves, halves).reshape(R, 4 * R)


def split_table():
    table = child_table().astype(np.float32)
    high = table.astype(jnp.bfloat16)
    low = (table - high.astype(np.float32)).astype(jnp.bfloat16)
    return np.concatenate([high, low, high], axis=1)


def offsets():
    c = nodes()
    parent = SIDE / 2 - 0.5 + SIDE / 2 * c
    child = np.concatenate([SIDE * u / 2 + SIDE / 4 - 0.5 + SIDE / 4 * c for u in (0, 1)])
    return child, parent


def centre_rows(targets):
    a = np.arange(targets)
    x1 = (2 * WIDTH * (a // COLS) + WIDTH - 1) / (2 * GRID)
    x2 = (2 * WIDTH * (a % COLS) + WIDTH - 1) / (2 * GRID)
    c1 = (2 + np.sin(16 * np.pi * x1) * np.sin(16 * np.pi * x2)) / 16
    c2 = (2 + np.cos(16 * np.pi * x1) * np.cos(16 * np.pi * x2)) / 16
    child, parent = offsets()
    rows = [np.stack([c1, c2] + [np.zeros(targets)] * 6)]
    for o in (child, parent):
        for x in (x1, x2):
            turn = o[:, None] * x[None, :]
            rows.append(turn - np.floor(turn))
    return np.concatenate(rows).astype(np.float32)


def offset_columns():
    child, parent = offsets()
    return np.broadcast_to(np.concatenate([child, parent])[:, None], (3 * Q, LANES)).astype(np.float32)


def half_turn(phase):
    r = phase - ((phase + WHOLE) - WHOLE)
    q = r * r
    s = SIN[3]
    for coefficient in SIN[2::-1]:
        s = s * q + coefficient
    s = s * r
    c = COS[3]
    for coefficient in COS[2::-1]:
        c = c * q + coefficient
    return 1.0 - s * s, s * c


def exact_turn(r):
    q = r * r
    s, c = FINE_SIN[-1], FINE_COS[-1]
    for coefficient in FINE_SIN[-2::-1]:
        s = s * q + coefficient
    for coefficient in FINE_COS[-2::-1]:
        c = c * q + coefficient
    s = s * r
    return jnp.where(s * s < 1.0, 1.0 - s * s, c * c - 1.0), s * c


def root(square):
    return square * lax.rsqrt(square)


def corner(own_boxes, box):
    position = lax.axis_index("grp") * lax.axis_size("dev") + lax.axis_index("dev")
    box_id = position * own_boxes + box
    return (box_id // ROW) * SIDE - GRID // 2, (box_id % ROW) * SIDE - GRID // 2


def outer(column, tile):
    return jnp.concatenate([column[j : j + 1] + tile for j in range(Q)], axis=0)


def source_box(own_boxes, targets, parents, b, weights_ref, table_ref, centre_ref, offset_ref, delta_ref):
    k1, k2 = corner(own_boxes, b)
    k1f, k2f = k1.astype(F32), k2.astype(F32)
    offs = offset_ref[...]
    for g in range(targets // LANES):
        lanes = slice(g * LANES, (g + 1) * LANES)
        lane = lax.broadcasted_iota(jnp.int32, (1, LANES), 1)
        box = lane + g * LANES
        h1 = 2 * WIDTH * (box // COLS) + WIDTH - 1
        h2 = 2 * WIDTH * (box % COLS) + WIDTH - 1
        whole = ((h1 * k1 + h2 * k2) & (2 * GRID - 1)).astype(F32) * (1.0 / (2 * GRID))
        c1 = centre_ref[0:1, lanes]
        c2 = centre_ref[1:2, lanes]
        first = c1 * (k1f + offs)
        first = first * first
        second = c2 * (k2f + offs)
        second = second * second
        turn1 = centre_ref[8 : 8 + 2 * Q, lanes]
        turn2 = centre_ref[8 + 2 * Q : 8 + 4 * Q, lanes] + whole
        back1 = centre_ref[8 + 4 * Q : 8 + 5 * Q, lanes]
        back2 = centre_ref[8 + 5 * Q : 8 + 6 * Q, lanes] + whole
        parent_lane = (g * (COLS // 2)) % LANES + (lane % COLS) // 2
        pick = jnp.broadcast_to(parent_lane, (R, LANES))
        start = (g * (COLS // 2)) // LANES * LANES
        high, low = [], []
        for u in range(2):
            for v in range(2):
                one, two = slice(u * Q, (u + 1) * Q), slice(v * Q, (v + 1) * Q)
                phase = root(outer(first[one], second[two])) + outer(turn1[one], turn2[two])
                cosine, sine = half_turn(phase)
                spread = []
                for z in range(2):
                    w = weights_ref[z, b, 2 * u + v, :, start : min(start + LANES, parents)]
                    if w.shape[1] < LANES:
                        w = jnp.concatenate([w] * (LANES // w.shape[1]), axis=1)
                    spread.append(jnp.take_along_axis(w, pick, axis=1, mode="promise_in_bounds"))
                wr, wi = spread
                both = jnp.concatenate([wr * cosine + wi * sine, wi * cosine - wr * sine], axis=1)
                top = both.astype(BF16)
                high.append(top)
                low.append((both - top.astype(F32)).astype(BF16))
        moved = jnp.concatenate(high + high + low, axis=0)
        interp = jnp.dot(table_ref[...], moved, preferred_element_type=F32)
        ir, ii = interp[:, :LANES], interp[:, LANES:]
        parent = slice(2 * Q, 3 * Q)
        phase = root(outer(first[parent], second[parent])) + outer(back1, back2)
        cosine, sine = half_turn(phase)
        for z, part in enumerate((ir * cosine - ii * sine, ii * cosine + ir * sine)):
            top = part.astype(BF16)
            delta_ref[b, z * R : (z + 1) * R, lanes] = top
            delta_ref[b, z * R : (z + 1) * R, targets + g * LANES : targets + (g + 1) * LANES] = (
                part - top.astype(F32)
            ).astype(BF16)


def row_facts(targets, c, span, facts, firsts, ends):
    row = lax.broadcasted_iota(jnp.int32, (span, targets), 0) + c * span
    hot = jnp.where((firsts <= row) & (row < ends), 1.0, 0.0).astype(BF16)
    here = lax.dot_general(facts, hot, CONTRACT, preferred_element_type=F32).astype(jnp.int32)
    place = lax.broadcasted_iota(jnp.int32, (1, span), 1) + c * span
    rank = place - (here[2 * RT + 2 : 2 * RT + 3] * LANES + here[2 * RT + 3 : 2 * RT + 4])
    mine = lax.broadcasted_iota(jnp.int32, (RT, span), 0) == rank
    p1 = jnp.sum(jnp.where(mine, here[:RT], 0), axis=0, keepdims=True)
    p2 = jnp.sum(jnp.where(mine, here[RT : 2 * RT], 0), axis=0, keepdims=True)
    h1 = here[2 * RT : 2 * RT + 1] * WIDTH + p1
    h2 = here[2 * RT + 1 : 2 * RT + 2] * WIDTH + p2
    points = jnp.concatenate([h1, h2], axis=0)
    angle = ((8 * points) & (GRID - 1)).astype(F32) * (1.0 / GRID)
    cosines, sines = exact_turn(angle - jnp.where(angle > 0.5, 1.0, 0.0))
    c1 = (2.0 + sines[0:1] * sines[1:2]) * (1.0 / 16)
    c2 = (2.0 + cosines[0:1] * cosines[1:2]) * (1.0 / 16)
    return hot, jnp.concatenate([points.astype(F32), c1, c2], axis=0)


def skeleton_rows(own_boxes, boxes, span, hot, point, delta_ref, offs):
    twice = jnp.concatenate([hot, hot], axis=1)
    h1, h2 = point[0:1].astype(jnp.int32), point[1:2].astype(jnp.int32)
    c1, c2 = point[2:3], point[3:4]
    turn1 = point[0:1] * (1.0 / GRID) * offs
    turn1 = turn1 - jnp.floor(turn1)
    turn2 = point[1:2] * (1.0 / GRID) * offs
    turn2 = turn2 - jnp.floor(turn2)
    first = c1 * (corner(own_boxes, 0)[0].astype(F32) + offs)
    first = first * first
    sums = []
    for b in boxes:
        k1, k2 = corner(own_boxes, b)
        picked = lax.dot_general(delta_ref[b], twice, CONTRACT, preferred_element_type=F32)
        wr, wi = picked[:R], picked[R:]
        whole = ((h1 * k1 + h2 * k2) & (GRID - 1)).astype(F32) * (1.0 / GRID)
        second = c2 * (k2.astype(F32) + offs)
        second = second * second
        phase = root(outer(first, second)) + outer(turn1, turn2 + whole)
        cosine, sine = half_turn(phase)
        real = wr * cosine - wi * sine
        imag = wr * sine + wi * cosine
        sums.append((jnp.sum(real.reshape(Q, Q, span), axis=0), jnp.sum(imag.reshape(Q, Q, span), axis=0)))
    return jnp.concatenate(
        [
            jnp.sum(sums[n][z] + sums[n + 1][z], axis=0, keepdims=True)
            for z in range(2)
            for n in range(0, len(boxes), 2)
        ],
        axis=0,
    )


def kernel(
    own_boxes, targets, parents, devices, depth,
    weights_hbm, pivots_hbm, ranks_hbm, owner_hbm, table_hbm, centre_hbm, offset_hbm, out_ref,
    weights, table, centre, offset, ranks_row, owner_row, all_pivots, delta, begin_row, stop_row, chunk_row, chunks,
    hots, points, compact, places, rows, got, mixed,
    weights_sem, const_sem, begin_sem, pivot_send, pivot_recv, rows_send, rows_recv,
):
    me = lax.axis_index("grp") * depth + lax.axis_index("dev")
    span = 2 * LANES
    spans = targets * RMEAN // span

    def device(index):
        return (lax.div(index, depth), lax.rem(index, depth))

    barrier = pltpu.get_barrier_semaphore()

    def greet(j, carry):
        pl.semaphore_signal(
            barrier, inc=1, device_id=device(lax.rem(me + j, devices)), device_id_type=pl.DeviceIdType.MESH
        )
        return carry

    pairs = [
        (ranks_hbm, ranks_row),
        (owner_hbm, owner_row),
        (table_hbm, table),
        (centre_hbm, centre),
        (offset_hbm, offset),
        (pivots_hbm, all_pivots.at[me]),
    ]
    consts = [pltpu.make_async_copy(far, near, const_sem.at[n]) for n, (far, near) in enumerate(pairs)]
    loads = [
        pltpu.make_async_copy(weights_hbm.at[:, b], weights.at[:, b], weights_sem.at[b]) for b in range(own_boxes)
    ]
    for copy in consts + loads:
        copy.start()
    lax.fori_loop(1, devices, greet, 0)
    for copy in consts:
        copy.wait()

    ranks = ranks_row[...]
    owners = owner_row[...]
    rank_down = jnp.broadcast_to(ranks, (targets, targets)).T
    owner_down = jnp.broadcast_to(owners, (targets, targets)).T
    slots = lax.broadcasted_iota(jnp.int32, (1, targets), 1)
    firsts = jnp.sum(jnp.where(owner_down < owners, rank_down, 0), axis=0, keepdims=True)
    ends = firsts + ranks
    begins = jnp.sum(jnp.where(owner_down < slots, rank_down, 0), axis=0, keepdims=True)
    begin_row[...] = begins
    stop_row[...] = jnp.sum(jnp.where(owner_down <= slots, rank_down, 0), axis=0, keepdims=True)
    chunk_row[...] = jnp.minimum(begins // LANES, 2 * spans - 1)
    to_scalars = pltpu.make_async_copy(chunk_row, chunks, begin_sem)
    to_scalars.start()

    def pivot_copy(target, source):
        return pltpu.make_async_remote_copy(
            src_ref=pivots_hbm,
            dst_ref=all_pivots.at[source],
            send_sem=pivot_send,
            recv_sem=pivot_recv,
            device_id=device(target),
            device_id_type=pl.DeviceIdType.MESH,
        )

    def send_pivots(j, carry):
        pivot_copy(lax.rem(me + j, devices), me).start()
        return carry

    def one_box(b, carry):
        pltpu.make_async_copy(weights_hbm.at[:, b], weights.at[:, b], weights_sem.at[b]).wait()
        source_box(own_boxes, targets, parents, b, weights, table, centre, offset, delta)
        return carry

    lax.fori_loop(0, 2, one_box, 0)
    pl.semaphore_wait(barrier, devices - 1)
    lax.fori_loop(1, devices, send_pivots, 0)
    lax.fori_loop(2, own_boxes, one_box, 0)

    boxes = LANES // RT
    groups = targets // devices // boxes
    tall = own_boxes // 2
    down = lax.broadcasted_iota(jnp.int32, (tall * groups, LANES), 0)
    lane = lax.broadcasted_iota(jnp.int32, (tall * groups, LANES), 1)
    opening = (down // tall) * boxes
    slot_here = opening + lane // RT
    per_tile = LANES // (groups * boxes)

    def one_tile(n, carry):
        for m in range(per_tile):
            spot = pl.ds(pl.multiple_of(n * LANES, LANES), LANES)
            first = jnp.broadcast_to(begin_row[:, spot], lane.shape)
            last = jnp.broadcast_to(stop_row[:, spot], lane.shape)
            tile_slot = slot_here + m * groups * boxes
            low = jnp.take_along_axis(first, tile_slot, axis=1, mode="promise_in_bounds")
            high = jnp.take_along_axis(last, tile_slot, axis=1, mode="promise_in_bounds")
            start = jnp.take_along_axis(first, opening + m * groups * boxes, axis=1, mode="promise_in_bounds")
            index = low + (lane & (RT - 1))
            places[n * per_tile + m] = jnp.where(index < high, index - (start & -LANES), -1)
        return carry

    lax.fori_loop(0, targets // LANES, one_tile, 0)
    to_scalars.wait()

    def drain(block, send, receive):
        copy = pltpu.make_async_remote_copy(
            src_ref=block,
            dst_ref=block,
            send_sem=send,
            recv_sem=receive,
            device_id=device(lax.rem(me + 1, devices)),
            device_id_type=pl.DeviceIdType.MESH,
        )
        copy.wait_send()
        copy.wait_recv()

    others = pl.ds(0, devices - 1)
    drain(all_pivots.at[others], pivot_send, pivot_recv)
    columns = all_pivots[...].reshape(targets, RT).astype(F32).T.astype(jnp.int32)
    facts = jnp.concatenate(
        [columns // WIDTH, columns % WIDTH, slots // COLS, slots % COLS, firsts // LANES, firsts % LANES]
        + [jnp.zeros((12, targets), jnp.int32)],
        axis=0,
    )
    facts = facts.astype(F32).astype(BF16)
    offs = offset[2 * Q : 3 * Q]
    offs = jnp.concatenate([offs, offs], axis=1)

    def one_fact(c, carry):
        hot, point = row_facts(targets, c, span, facts, firsts, ends)
        hots[c] = hot
        points[c, 0:4] = point
        return carry

    lax.fori_loop(0, spans, one_fact, 0, unroll=5 if spans % 5 == 0 else 1)
    compact[2 * spans] = jnp.zeros((tall * groups, LANES), F32)

    def rows_copy(half, target, source):
        return pltpu.make_async_remote_copy(
            src_ref=rows.at[half, target],
            dst_ref=got.at[half, source],
            send_sem=rows_send,
            recv_sem=rows_recv,
            device_id=device(target),
            device_id_type=pl.DeviceIdType.MESH,
        )

    for half in range(2):
        mine = range(half * own_boxes // 2, (half + 1) * own_boxes // 2)

        def one_span(c, carry):
            block = skeleton_rows(own_boxes, mine, span, hots[c], points[c], delta, offs)
            block = jnp.concatenate([block] * groups, axis=0)
            compact[2 * c] = block[:, :LANES]
            compact[2 * c + 1] = block[:, LANES:]
            return carry

        def place_rows(owner, carry):
            slot = owner * groups * boxes
            near, far = compact[chunks[0, slot]], compact[chunks[0, slot] + 1]
            for n in range(1, groups):
                chunk = chunks[0, slot + n * boxes]
                near = jnp.where(down >= n * tall, compact[chunk], near)
                far = jnp.where(down >= n * tall, compact[chunk + 1], far)
            place = places[owner]
            within = place & (LANES - 1)
            near = jnp.take_along_axis(near, within, axis=1, mode="promise_in_bounds")
            far = jnp.take_along_axis(far, within, axis=1, mode="promise_in_bounds")
            rows[half, owner] = jnp.where(place < 0, 0.0, jnp.where(place >= LANES, far, near))
            return carry

        def send_rows(j, carry):
            rows_copy(half, lax.rem(me + j, devices), me).start()
            return carry

        lax.fori_loop(0, spans, one_span, 0)
        lax.fori_loop(0, devices, place_rows, 0, unroll=8)
        lax.fori_loop(1, devices, send_rows, 0)
        got[half, me] = rows[half, me]

    drain(got.at[:, others], rows_send, rows_recv)

    pair = ROW // own_boxes
    few = own_boxes // 4

    def mix(n, carry):
        sums = []
        for k in (2 * n, 2 * n + 1):
            upper = lax.div(k, pair) * 2 * pair + lax.rem(k, pair)
            sums += [got[half, upper] + got[half, upper + pair] for half in range(2)]
        for part in range(2 * groups):
            lines = slice(part * few, (part + 1) * few)
            mixed[part, pl.ds(pl.multiple_of(n * 4 * few, 4 * few), 4 * few)] = jnp.concatenate(
                [block[lines] for block in sums], axis=0
            )
        return carry

    lax.fori_loop(0, devices // 4, mix, 0, unroll=4)
    for n in range(groups):
        for z in range(2):
            turned = mixed[2 * n + z].T
            for k in range(boxes):
                out_ref[z, :, n * boxes + k, :] = turned[k * RT : (k + 1) * RT]


def local(child_weights, pivots, ranks, owner_slot):
    depth = lax.axis_size("dev")
    devices = lax.axis_size("grp") * depth
    own_boxes = child_weights.shape[1]
    parents = child_weights.shape[4]
    targets = ranks.shape[0]
    groups = targets // devices * RT // LANES
    tall = own_boxes // 2 * groups
    sources = devices * own_boxes // 4
    spans = targets * RMEAN // (2 * LANES)
    anywhere = pl.BlockSpec(memory_space=pl.ANY)
    table, centre, offs = split_table(), centre_rows(targets), offset_columns()
    dma = pltpu.SemaphoreType.DMA
    return pl.pallas_call(
        lambda *refs: kernel(own_boxes, targets, parents, devices, depth, *refs),
        in_specs=[anywhere] * 7,
        out_specs=pl.BlockSpec(memory_space=pltpu.VMEM),
        out_shape=jax.ShapeDtypeStruct((2, RT, targets // devices, sources), F32),
        scratch_shapes=[
            pltpu.VMEM(child_weights.shape, F32),
            pltpu.VMEM(table.shape, BF16),
            pltpu.VMEM(centre.shape, F32),
            pltpu.VMEM(offs.shape, F32),
            pltpu.VMEM((1, targets), jnp.int32),
            pltpu.VMEM((1, targets), jnp.int32),
            pltpu.VMEM((devices,) + pivots.shape, jnp.int32),
            pltpu.VMEM((own_boxes, 2 * R, 2 * targets), BF16),
            pltpu.VMEM((1, targets), jnp.int32),
            pltpu.VMEM((1, targets), jnp.int32),
            pltpu.VMEM((1, targets), jnp.int32),
            pltpu.SMEM((1, targets), jnp.int32),
            pltpu.VMEM((spans, 2 * LANES, targets), BF16),
            pltpu.VMEM((spans, 8, 2 * LANES), F32),
            pltpu.VMEM((2 * spans + 1, tall, LANES), F32),
            pltpu.VMEM((devices, tall, LANES), jnp.int32),
            pltpu.VMEM((2, devices, tall, LANES), F32),
            pltpu.VMEM((2, devices, tall, LANES), F32),
            pltpu.VMEM((2 * groups, sources, LANES), F32),
            dma((own_boxes,)),
            dma((6,)),
            dma,
            dma,
            dma,
            dma,
            dma,
        ],
        compiler_params=pltpu.CompilerParams(
            collective_id=0, has_side_effects=True, vmem_limit_bytes=60 << 20
        ),
    )(child_weights, pivots, ranks.reshape(1, targets), owner_slot.reshape(1, targets), table, centre, offs)


def solution(mesh):
    in_specs = (P(None, ("grp", "dev"), None, None, None), P(("grp", "dev"), None), P(), P())
    out_specs = P(None, None, ("grp", "dev"), None)
    return jax.shard_map(local, mesh=mesh, in_specs=in_specs, out_specs=out_specs, check_vma=False)
```

```python
import math

import jax
import jax.numpy as jnp
import numpy as np
from jax import lax
from jax.experimental import pallas as pl
from jax.experimental.pallas import tpu as pltpu
from jax.sharding import PartitionSpec as P

GRID = 2048
Q = 8
RT = 32
RMEAN = 10
SIDE = GRID // 32
WIDTH = GRID // 64
ROW = GRID // 64
COLS = GRID // 32
LANES = 128
WHOLE = 1.5 * 2**23
R = Q * Q

SIN = (4.442867904603554, -7.30744348201647, 3.594788644821573, -0.7843755040132807)
COS = (1.414204082132758, -6.977642209183305, 5.715240371096478, -1.7283548501332477)
FINE_SIN = (4.442882938082702, -7.308249478180419, 3.6064755519164122, -0.8474705853915653, 0.1160367907993074, -0.009939639006380334)
FINE_COS = (1.4142135623720344, -6.97886419922267, 5.739885708281956, -1.8883460761614363, 0.3328004285822709, -0.03645323263485946, 0.002602159860467781)

F32 = jnp.float32
BF16 = jnp.bfloat16
CONTRACT = (((1,), (1,)), ((), ()))


def nodes():
    return np.cos(np.pi * (2.0 * np.arange(Q) + 1.0) / (2.0 * Q))


def lagrange(at, points):
    out = np.ones((Q, Q))
    for t in range(Q):
        for k in range(Q):
            if k != t:
                out[t] *= (points - at[k]) / (at[t] - at[k])
    return out


def child_table():
    c = nodes()
    halves = np.stack([lagrange(c, u - 0.5 + 0.5 * c) for u in (0.0, 1.0)])
    return np.einsum("uaj,vbk->abuvjk", halves, halves).reshape(R, 4 * R)


def split_table():
    table = child_table().astype(np.float32)
    high = table.astype(jnp.bfloat16)
    low = (table - high.astype(np.float32)).astype(jnp.bfloat16)
    return np.concatenate([high, low], axis=0)


def offsets():
    c = nodes()
    parent = SIDE / 2 - 0.5 + SIDE / 2 * c
    child = np.concatenate([SIDE * u / 2 + SIDE / 4 - 0.5 + SIDE / 4 * c for u in (0, 1)])
    return child, parent


def centre_rows(targets):
    a = np.arange(targets)
    x1 = (2 * WIDTH * (a // COLS) + WIDTH - 1) / (2 * GRID)
    x2 = (2 * WIDTH * (a % COLS) + WIDTH - 1) / (2 * GRID)
    c1 = (2 + np.sin(16 * np.pi * x1) * np.sin(16 * np.pi * x2)) / 16
    c2 = (2 + np.cos(16 * np.pi * x1) * np.cos(16 * np.pi * x2)) / 16
    child, parent = offsets()
    rows = [np.stack([c1, c2] + [np.zeros(targets)] * 6)]
    for o in (child, parent):
        for x in (x1, x2):
            turn = o[:, None] * x[None, :]
            rows.append(turn - np.floor(turn))
    return np.concatenate(rows).astype(np.float32)


def offset_columns():
    child, parent = offsets()
    return np.broadcast_to(np.concatenate([child, parent])[:, None], (3 * Q, LANES)).astype(np.float32)


def half_turn(phase):
    r = phase - ((phase + WHOLE) - WHOLE)
    q = r * r
    s = SIN[3]
    for coefficient in SIN[2::-1]:
        s = s * q + coefficient
    s = s * r
    c = COS[3]
    for coefficient in COS[2::-1]:
        c = c * q + coefficient
    return 1.0 - s * s, s * c


def exact_turn(r):
    q = r * r
    s, c = FINE_SIN[-1], FINE_COS[-1]
    for coefficient in FINE_SIN[-2::-1]:
        s = s * q + coefficient
    for coefficient in FINE_COS[-2::-1]:
        c = c * q + coefficient
    s = s * r
    return jnp.where(s * s < 1.0, 1.0 - s * s, c * c - 1.0), s * c


def root(square):
    return square * lax.rsqrt(square)


def corner(own_boxes, box):
    position = lax.axis_index("grp") * lax.axis_size("dev") + lax.axis_index("dev")
    box_id = position * own_boxes + box
    return (box_id // ROW) * SIDE - GRID // 2, (box_id % ROW) * SIDE - GRID // 2


def outer(column, tile):
    return jnp.concatenate([column[j : j + 1] + tile for j in range(Q)], axis=0)


def source_box(own_boxes, targets, parents, b, weights_ref, table_ref, centre_ref, offset_ref, delta_ref):
    k1, k2 = corner(own_boxes, b)
    k1f, k2f = k1.astype(F32), k2.astype(F32)
    offs = offset_ref[...]
    for g in range(targets // LANES):
        lanes = slice(g * LANES, (g + 1) * LANES)
        lane = lax.broadcasted_iota(jnp.int32, (1, LANES), 1)
        box = lane + g * LANES
        h1 = 2 * WIDTH * (box // COLS) + WIDTH - 1
        h2 = 2 * WIDTH * (box % COLS) + WIDTH - 1
        whole = ((h1 * k1 + h2 * k2) & (2 * GRID - 1)).astype(F32) * (1.0 / (2 * GRID))
        c1 = centre_ref[0:1, lanes]
        c2 = centre_ref[1:2, lanes]
        first = c1 * (k1f + offs)
        first = first * first
        second = c2 * (k2f + offs)
        second = second * second
        turn1 = centre_ref[8 : 8 + 2 * Q, lanes]
        turn2 = centre_ref[8 + 2 * Q : 8 + 4 * Q, lanes] + whole
        back1 = centre_ref[8 + 4 * Q : 8 + 5 * Q, lanes]
        back2 = centre_ref[8 + 5 * Q : 8 + 6 * Q, lanes] + whole
        parent_lane = (g * (COLS // 2)) % LANES + (lane % COLS) // 2
        pick = jnp.broadcast_to(parent_lane, (R, LANES))
        start = (g * (COLS // 2)) // LANES * LANES
        high, low = [], []
        for u in range(2):
            for v in range(2):
                one, two = slice(u * Q, (u + 1) * Q), slice(v * Q, (v + 1) * Q)
                phase = root(outer(first[one], second[two])) + outer(turn1[one], turn2[two])
                cosine, sine = half_turn(phase)
                spread = []
                for z in range(2):
                    w = weights_ref[z, b, 2 * u + v, :, start : min(start + LANES, parents)]
                    if w.shape[1] < LANES:
                        w = jnp.concatenate([w] * (LANES // w.shape[1]), axis=1)
                    spread.append(jnp.take_along_axis(w, pick, axis=1, mode="promise_in_bounds"))
                wr, wi = spread
                both = jnp.concatenate([wr * cosine + wi * sine, wi * cosine - wr * sine], axis=1)
                top = both.astype(BF16)
                high.append(top)
                low.append((both - top.astype(F32)).astype(BF16))
        wide = jnp.dot(table_ref[...], jnp.concatenate(high, axis=0), preferred_element_type=F32)
        fine = jnp.dot(table_ref[:R], jnp.concatenate(low, axis=0), preferred_element_type=F32)
        interp = wide[:R] + (wide[R:] + fine)
        ir, ii = interp[:, :LANES], interp[:, LANES:]
        parent = slice(2 * Q, 3 * Q)
        phase = root(outer(first[parent], second[parent])) + outer(back1, back2)
        cosine, sine = half_turn(phase)
        for z, part in enumerate((ir * cosine - ii * sine, ii * cosine + ir * sine)):
            top = part.astype(BF16)
            delta_ref[b, z * R : (z + 1) * R, lanes] = top
            delta_ref[b, z * R : (z + 1) * R, targets + g * LANES : targets + (g + 1) * LANES] = (
                part - top.astype(F32)
            ).astype(BF16)


def row_facts(targets, c, span, facts, firsts, ends):
    row = lax.broadcasted_iota(jnp.int32, (span, targets), 0) + c * span
    hot = jnp.where((firsts <= row) & (row < ends), 1.0, 0.0).astype(BF16)
    here = lax.dot_general(facts, hot, CONTRACT, preferred_element_type=F32).astype(jnp.int32)
    place = lax.broadcasted_iota(jnp.int32, (1, span), 1) + c * span
    rank = place - (here[2 * RT + 2 : 2 * RT + 3] * LANES + here[2 * RT + 3 : 2 * RT + 4])
    mine = lax.broadcasted_iota(jnp.int32, (RT, span), 0) == rank
    p1 = jnp.sum(jnp.where(mine, here[:RT], 0), axis=0, keepdims=True)
    p2 = jnp.sum(jnp.where(mine, here[RT : 2 * RT], 0), axis=0, keepdims=True)
    h1 = here[2 * RT : 2 * RT + 1] * WIDTH + p1
    h2 = here[2 * RT + 1 : 2 * RT + 2] * WIDTH + p2
    points = jnp.concatenate([h1, h2], axis=0)
    angle = ((8 * points) & (GRID - 1)).astype(F32) * (1.0 / GRID)
    cosines, sines = exact_turn(angle - jnp.where(angle > 0.5, 1.0, 0.0))
    c1 = (2.0 + sines[0:1] * sines[1:2]) * (1.0 / 16)
    c2 = (2.0 + cosines[0:1] * cosines[1:2]) * (1.0 / 16)
    return hot, jnp.concatenate([points.astype(F32), c1, c2], axis=0)


def skeleton_rows(own_boxes, boxes, span, hot, point, delta_ref, offs):
    twice = jnp.concatenate([hot, hot], axis=1)
    h1, h2 = point[0:1].astype(jnp.int32), point[1:2].astype(jnp.int32)
    c1, c2 = point[2:3], point[3:4]
    turn1 = point[0:1] * (1.0 / GRID) * offs
    turn1 = turn1 - jnp.floor(turn1)
    turn2 = point[1:2] * (1.0 / GRID) * offs
    turn2 = turn2 - jnp.floor(turn2)
    first = c1 * (corner(own_boxes, 0)[0].astype(F32) + offs)
    first = first * first
    block = delta_ref[boxes[0] : boxes[-1] + 1].reshape(len(boxes) * 2 * R, twice.shape[1])
    picked = lax.dot_general(block, twice, CONTRACT, preferred_element_type=F32)
    sums = []
    for n, b in enumerate(boxes):
        k1, k2 = corner(own_boxes, b)
        at = 2 * R * n
        wr, wi = picked[at : at + R], picked[at + R : at + 2 * R]
        whole = ((h1 * k1 + h2 * k2) & (GRID - 1)).astype(F32) * (1.0 / GRID)
        second = c2 * (k2.astype(F32) + offs)
        second = second * second
        phase = root(outer(first, second)) + outer(turn1, turn2 + whole)
        cosine, sine = half_turn(phase)
        real = wr * cosine - wi * sine
        imag = wr * sine + wi * cosine
        sums.append((jnp.sum(real.reshape(Q, Q, span), axis=0), jnp.sum(imag.reshape(Q, Q, span), axis=0)))
    return jnp.concatenate(
        [
            jnp.sum(sums[n][z] + sums[n + 1][z], axis=0, keepdims=True)
            for z in range(2)
            for n in range(0, len(boxes), 2)
        ],
        axis=0,
    )


def kernel(
    own_boxes, targets, parents, devices, depth,
    weights_hbm, pivots_hbm, ranks_hbm, owner_hbm, table_hbm, centre_hbm, offset_hbm, out_ref,
    weights, table, centre, offset, ranks_row, owner_row, all_pivots, delta, begin_row, stop_row, chunk_row, chunks,
    hots, points, compact, places, rows, got, mixed,
    weights_sem, const_sem, begin_sem, pivot_send, pivot_recv, rows_send, rows_recv,
):
    me = lax.axis_index("grp") * depth + lax.axis_index("dev")
    span = 2 * LANES
    spans = targets * RMEAN // span

    def device(index):
        return (lax.div(index, depth), lax.rem(index, depth))

    barrier = pltpu.get_barrier_semaphore()

    def greet(j, carry):
        pl.semaphore_signal(
            barrier, inc=1, device_id=device(lax.rem(me + j, devices)), device_id_type=pl.DeviceIdType.MESH
        )
        return carry

    pairs = [
        (ranks_hbm, ranks_row),
        (owner_hbm, owner_row),
        (table_hbm, table),
        (centre_hbm, centre),
        (offset_hbm, offset),
        (pivots_hbm, all_pivots.at[me]),
    ]
    consts = [pltpu.make_async_copy(far, near, const_sem.at[n]) for n, (far, near) in enumerate(pairs)]
    loads = [
        pltpu.make_async_copy(weights_hbm.at[:, b], weights.at[:, b], weights_sem.at[b]) for b in range(own_boxes)
    ]
    for copy in consts + loads:
        copy.start()
    lax.fori_loop(1, devices, greet, 0)
    for copy in consts:
        copy.wait()

    ranks = ranks_row[...]
    owners = owner_row[...]
    rank_down = jnp.broadcast_to(ranks, (targets, targets)).T
    owner_down = jnp.broadcast_to(owners, (targets, targets)).T
    slots = lax.broadcasted_iota(jnp.int32, (1, targets), 1)
    firsts = jnp.sum(jnp.where(owner_down < owners, rank_down, 0), axis=0, keepdims=True)
    ends = firsts + ranks
    begins = jnp.sum(jnp.where(owner_down < slots, rank_down, 0), axis=0, keepdims=True)
    begin_row[...] = begins
    stop_row[...] = jnp.sum(jnp.where(owner_down <= slots, rank_down, 0), axis=0, keepdims=True)
    chunk_row[...] = jnp.minimum(begins // LANES, 2 * spans - 1)
    to_scalars = pltpu.make_async_copy(chunk_row, chunks, begin_sem)
    to_scalars.start()

    def pivot_copy(target, source):
        return pltpu.make_async_remote_copy(
            src_ref=pivots_hbm,
            dst_ref=all_pivots.at[source],
            send_sem=pivot_send,
            recv_sem=pivot_recv,
            device_id=device(target),
            device_id_type=pl.DeviceIdType.MESH,
        )

    def send_pivots(j, carry):
        pivot_copy(lax.rem(me + j, devices), me).start()
        return carry

    def one_box(b, carry):
        pltpu.make_async_copy(weights_hbm.at[:, b], weights.at[:, b], weights_sem.at[b]).wait()
        source_box(own_boxes, targets, parents, b, weights, table, centre, offset, delta)
        return carry

    lax.fori_loop(0, 2, one_box, 0)
    pl.semaphore_wait(barrier, devices - 1)
    lax.fori_loop(1, devices, send_pivots, 0)
    lax.fori_loop(2, own_boxes, one_box, 0)

    boxes = LANES // RT
    groups = targets // devices // boxes
    tall = own_boxes // 2
    down = lax.broadcasted_iota(jnp.int32, (tall * groups, LANES), 0)
    lane = lax.broadcasted_iota(jnp.int32, (tall * groups, LANES), 1)
    opening = (down // tall) * boxes
    slot_here = opening + lane // RT
    per_tile = LANES // (groups * boxes)

    def one_tile(n, carry):
        for m in range(per_tile):
            spot = pl.ds(pl.multiple_of(n * LANES, LANES), LANES)
            first = jnp.broadcast_to(begin_row[:, spot], lane.shape)
            last = jnp.broadcast_to(stop_row[:, spot], lane.shape)
            tile_slot = slot_here + m * groups * boxes
            low = jnp.take_along_axis(first, tile_slot, axis=1, mode="promise_in_bounds")
            high = jnp.take_along_axis(last, tile_slot, axis=1, mode="promise_in_bounds")
            start = jnp.take_along_axis(first, opening + m * groups * boxes, axis=1, mode="promise_in_bounds")
            index = low + (lane & (RT - 1))
            places[n * per_tile + m] = jnp.where(index < high, index - (start & -LANES), -1)
        return carry

    lax.fori_loop(0, targets // LANES, one_tile, 0)
    to_scalars.wait()

    def drain(block, send, receive):
        copy = pltpu.make_async_remote_copy(
            src_ref=block,
            dst_ref=block,
            send_sem=send,
            recv_sem=receive,
            device_id=device(lax.rem(me + 1, devices)),
            device_id_type=pl.DeviceIdType.MESH,
        )
        copy.wait_send()
        copy.wait_recv()

    others = pl.ds(0, devices - 1)
    drain(all_pivots.at[others], pivot_send, pivot_recv)
    columns = all_pivots[...].reshape(targets, RT).astype(F32).T.astype(jnp.int32)
    facts = jnp.concatenate(
        [columns // WIDTH, columns % WIDTH, slots // COLS, slots % COLS, firsts // LANES, firsts % LANES]
        + [jnp.zeros((12, targets), jnp.int32)],
        axis=0,
    )
    facts = facts.astype(F32).astype(BF16)
    offs = offset[2 * Q : 3 * Q]
    offs = jnp.concatenate([offs, offs], axis=1)

    def one_fact(c, carry):
        hot, point = row_facts(targets, c, span, facts, firsts, ends)
        hots[c] = hot
        points[c, 0:4] = point
        return carry

    lax.fori_loop(0, spans, one_fact, 0, unroll=5 if spans % 5 == 0 else 1)
    compact[2 * spans] = jnp.zeros((tall * groups, LANES), F32)

    def rows_copy(half, target, source):
        return pltpu.make_async_remote_copy(
            src_ref=rows.at[half, target],
            dst_ref=got.at[half, source],
            send_sem=rows_send,
            recv_sem=rows_recv,
            device_id=device(target),
            device_id_type=pl.DeviceIdType.MESH,
        )

    for half in range(2):
        mine = range(half * own_boxes // 2, (half + 1) * own_boxes // 2)

        def one_span(c, carry):
            block = skeleton_rows(own_boxes, mine, span, hots[c], points[c], delta, offs)
            block = jnp.concatenate([block] * groups, axis=0)
            compact[2 * c] = block[:, :LANES]
            compact[2 * c + 1] = block[:, LANES:]
            return carry

        def place_rows(owner, carry):
            slot = owner * groups * boxes
            near, far = compact[chunks[0, slot]], compact[chunks[0, slot] + 1]
            for n in range(1, groups):
                chunk = chunks[0, slot + n * boxes]
                near = jnp.where(down >= n * tall, compact[chunk], near)
                far = jnp.where(down >= n * tall, compact[chunk + 1], far)
            place = places[owner]
            within = place & (LANES - 1)
            near = jnp.take_along_axis(near, within, axis=1, mode="promise_in_bounds")
            far = jnp.take_along_axis(far, within, axis=1, mode="promise_in_bounds")
            rows[half, owner] = jnp.where(place < 0, 0.0, jnp.where(place >= LANES, far, near))
            return carry

        def send_rows(j, carry):
            rows_copy(half, lax.rem(me + j, devices), me).start()
            return carry

        lax.fori_loop(0, spans, one_span, 0)
        lax.fori_loop(0, devices, place_rows, 0, unroll=8)
        lax.fori_loop(1, devices, send_rows, 0)
        got[half, me] = rows[half, me]

    drain(got.at[:, others], rows_send, rows_recv)

    pair = ROW // own_boxes
    few = own_boxes // 4

    def mix(n, carry):
        sums = []
        for k in (2 * n, 2 * n + 1):
            upper = lax.div(k, pair) * 2 * pair + lax.rem(k, pair)
            sums += [got[half, upper] + got[half, upper + pair] for half in range(2)]
        for part in range(2 * groups):
            lines = slice(part * few, (part + 1) * few)
            mixed[part, pl.ds(pl.multiple_of(n * 4 * few, 4 * few), 4 * few)] = jnp.concatenate(
                [block[lines] for block in sums], axis=0
            )
        return carry

    lax.fori_loop(0, devices // 4, mix, 0, unroll=4)
    for n in range(groups):
        for z in range(2):
            turned = mixed[2 * n + z].T
            for k in range(boxes):
                out_ref[z, :, n * boxes + k, :] = turned[k * RT : (k + 1) * RT]


def local(child_weights, pivots, ranks, owner_slot):
    depth = lax.axis_size("dev")
    devices = lax.axis_size("grp") * depth
    own_boxes = child_weights.shape[1]
    parents = child_weights.shape[4]
    targets = ranks.shape[0]
    groups = targets // devices * RT // LANES
    tall = own_boxes // 2 * groups
    sources = devices * own_boxes // 4
    spans = targets * RMEAN // (2 * LANES)
    anywhere = pl.BlockSpec(memory_space=pl.ANY)
    table, centre, offs = split_table(), centre_rows(targets), offset_columns()
    dma = pltpu.SemaphoreType.DMA
    return pl.pallas_call(
        lambda *refs: kernel(own_boxes, targets, parents, devices, depth, *refs),
        in_specs=[anywhere] * 7,
        out_specs=pl.BlockSpec(memory_space=pltpu.VMEM),
        out_shape=jax.ShapeDtypeStruct((2, RT, targets // devices, sources), F32),
        scratch_shapes=[
            pltpu.VMEM(child_weights.shape, F32),
            pltpu.VMEM(table.shape, BF16),
            pltpu.VMEM(centre.shape, F32),
            pltpu.VMEM(offs.shape, F32),
            pltpu.VMEM((1, targets), jnp.int32),
            pltpu.VMEM((1, targets), jnp.int32),
            pltpu.VMEM((devices,) + pivots.shape, jnp.int32),
            pltpu.VMEM((own_boxes, 2 * R, 2 * targets), BF16),
            pltpu.VMEM((1, targets), jnp.int32),
            pltpu.VMEM((1, targets), jnp.int32),
            pltpu.VMEM((1, targets), jnp.int32),
            pltpu.SMEM((1, targets), jnp.int32),
            pltpu.VMEM((spans, 2 * LANES, targets), BF16),
            pltpu.VMEM((spans, 8, 2 * LANES), F32),
            pltpu.VMEM((2 * spans + 1, tall, LANES), F32),
            pltpu.VMEM((devices, tall, LANES), jnp.int32),
            pltpu.VMEM((2, devices, tall, LANES), F32),
            pltpu.VMEM((2, devices, tall, LANES), F32),
            pltpu.VMEM((2 * groups, sources, LANES), F32),
            dma((own_boxes,)),
            dma((6,)),
            dma,
            dma,
            dma,
            dma,
            dma,
        ],
        compiler_params=pltpu.CompilerParams(
            collective_id=0, has_side_effects=True, vmem_limit_bytes=60 << 20
        ),
    )(child_weights, pivots, ranks.reshape(1, targets), owner_slot.reshape(1, targets), table, centre, offs)


def solution(mesh):
    in_specs = (P(None, ("grp", "dev"), None, None, None), P(("grp", "dev"), None), P(), P())
    out_specs = P(None, None, ("grp", "dev"), None)
    return jax.shard_map(local, mesh=mesh, in_specs=in_specs, out_specs=out_specs, check_vma=False)
```

```python
import math

import jax
import jax.numpy as jnp
import numpy as np
from jax import lax
from jax.experimental import pallas as pl
from jax.experimental.pallas import tpu as pltpu
from jax.sharding import PartitionSpec as P

GRID = 2048
Q = 8
RT = 32
RMEAN = 10
SIDE = GRID // 32
WIDTH = GRID // 64
ROW = GRID // 64
COLS = GRID // 32
LANES = 128
WHOLE = 1.5 * 2**23
R = Q * Q

SIN = (4.442867904603554, -7.30744348201647, 3.594788644821573, -0.7843755040132807)
COS = (1.414204082132758, -6.977642209183305, 5.715240371096478, -1.7283548501332477)
FINE_SIN = (4.442882938082702, -7.308249478180419, 3.6064755519164122, -0.8474705853915653, 0.1160367907993074, -0.009939639006380334)
FINE_COS = (1.4142135623720344, -6.97886419922267, 5.739885708281956, -1.8883460761614363, 0.3328004285822709, -0.03645323263485946, 0.002602159860467781)

F32 = jnp.float32
BF16 = jnp.bfloat16
CONTRACT = (((1,), (1,)), ((), ()))


def nodes():
    return np.cos(np.pi * (2.0 * np.arange(Q) + 1.0) / (2.0 * Q))


def lagrange(at, points):
    out = np.ones((Q, Q))
    for t in range(Q):
        for k in range(Q):
            if k != t:
                out[t] *= (points - at[k]) / (at[t] - at[k])
    return out


def child_table():
    c = nodes()
    halves = np.stack([lagrange(c, u - 0.5 + 0.5 * c) for u in (0.0, 1.0)])
    return np.einsum("uaj,vbk->abuvjk", halves, halves).reshape(R, 4 * R)


def split_table():
    table = child_table().astype(np.float32)
    high = table.astype(jnp.bfloat16)
    low = (table - high.astype(np.float32)).astype(jnp.bfloat16)
    return np.concatenate([high, low], axis=0)


def offsets():
    c = nodes()
    parent = SIDE / 2 - 0.5 + SIDE / 2 * c
    child = np.concatenate([SIDE * u / 2 + SIDE / 4 - 0.5 + SIDE / 4 * c for u in (0, 1)])
    return child, parent


def centre_rows(targets):
    a = np.arange(targets)
    x1 = (2 * WIDTH * (a // COLS) + WIDTH - 1) / (2 * GRID)
    x2 = (2 * WIDTH * (a % COLS) + WIDTH - 1) / (2 * GRID)
    c1 = (2 + np.sin(16 * np.pi * x1) * np.sin(16 * np.pi * x2)) / 16
    c2 = (2 + np.cos(16 * np.pi * x1) * np.cos(16 * np.pi * x2)) / 16
    child, parent = offsets()
    rows = [np.stack([c1, c2] + [np.zeros(targets)] * 6)]
    for o in (child, parent):
        for x in (x1, x2):
            turn = o[:, None] * x[None, :]
            rows.append(turn - np.floor(turn))
    return np.concatenate(rows).astype(np.float32)


def offset_columns():
    child, parent = offsets()
    return np.broadcast_to(np.concatenate([child, parent])[:, None], (3 * Q, LANES)).astype(np.float32)


def half_turn(phase):
    r = phase - ((phase + WHOLE) - WHOLE)
    q = r * r
    s = SIN[3]
    for coefficient in SIN[2::-1]:
        s = s * q + coefficient
    s = s * r
    c = COS[3]
    for coefficient in COS[2::-1]:
        c = c * q + coefficient
    return 1.0 - s * s, s * c


def exact_turn(r):
    q = r * r
    s, c = FINE_SIN[-1], FINE_COS[-1]
    for coefficient in FINE_SIN[-2::-1]:
        s = s * q + coefficient
    for coefficient in FINE_COS[-2::-1]:
        c = c * q + coefficient
    s = s * r
    return jnp.where(s * s < 1.0, 1.0 - s * s, c * c - 1.0), s * c


def root(square):
    return square * lax.rsqrt(square)


def corner(own_boxes, box):
    position = lax.axis_index("grp") * lax.axis_size("dev") + lax.axis_index("dev")
    box_id = position * own_boxes + box
    return (box_id // ROW) * SIDE - GRID // 2, (box_id % ROW) * SIDE - GRID // 2


def outer(column, tile):
    return jnp.concatenate([column[j : j + 1] + tile for j in range(Q)], axis=0)


def source_box(own_boxes, targets, parents, b, weights_ref, table_ref, centre_ref, offset_ref, delta_ref):
    k1, k2 = corner(own_boxes, b)
    k1f, k2f = k1.astype(F32), k2.astype(F32)
    offs = offset_ref[...]
    for g in range(targets // LANES):
        lanes = slice(g * LANES, (g + 1) * LANES)
        lane = lax.broadcasted_iota(jnp.int32, (1, LANES), 1)
        box = lane + g * LANES
        h1 = 2 * WIDTH * (box // COLS) + WIDTH - 1
        h2 = 2 * WIDTH * (box % COLS) + WIDTH - 1
        whole = ((h1 * k1 + h2 * k2) & (2 * GRID - 1)).astype(F32) * (1.0 / (2 * GRID))
        c1 = centre_ref[0:1, lanes]
        c2 = centre_ref[1:2, lanes]
        first = c1 * (k1f + offs)
        first = first * first
        second = c2 * (k2f + offs)
        second = second * second
        turn1 = centre_ref[8 : 8 + 2 * Q, lanes]
        turn2 = centre_ref[8 + 2 * Q : 8 + 4 * Q, lanes] + whole
        back1 = centre_ref[8 + 4 * Q : 8 + 5 * Q, lanes]
        back2 = centre_ref[8 + 5 * Q : 8 + 6 * Q, lanes] + whole
        parent_lane = (g * (COLS // 2)) % LANES + (lane % COLS) // 2
        pick = jnp.broadcast_to(parent_lane, (R, LANES))
        start = (g * (COLS // 2)) // LANES * LANES
        high, low = [], []
        for u in range(2):
            for v in range(2):
                one, two = slice(u * Q, (u + 1) * Q), slice(v * Q, (v + 1) * Q)
                phase = root(outer(first[one], second[two])) + outer(turn1[one], turn2[two])
                cosine, sine = half_turn(phase)
                spread = []
                for z in range(2):
                    w = weights_ref[z, b, 2 * u + v, :, start : min(start + LANES, parents)]
                    if w.shape[1] < LANES:
                        w = jnp.concatenate([w] * (LANES // w.shape[1]), axis=1)
                    spread.append(jnp.take_along_axis(w, pick, axis=1, mode="promise_in_bounds"))
                wr, wi = spread
                both = jnp.concatenate([wr * cosine + wi * sine, wi * cosine - wr * sine], axis=1)
                top = both.astype(BF16)
                high.append(top)
                low.append((both - top.astype(F32)).astype(BF16))
        wide = jnp.dot(table_ref[...], jnp.concatenate(high, axis=0), preferred_element_type=F32)
        fine = jnp.dot(table_ref[:R], jnp.concatenate(low, axis=0), preferred_element_type=F32)
        interp = wide[:R] + (wide[R:] + fine)
        ir, ii = interp[:, :LANES], interp[:, LANES:]
        parent = slice(2 * Q, 3 * Q)
        phase = root(outer(first[parent], second[parent])) + outer(back1, back2)
        cosine, sine = half_turn(phase)
        for z, part in enumerate((ir * cosine - ii * sine, ii * cosine + ir * sine)):
            top = part.astype(BF16)
            delta_ref[b, z * R : (z + 1) * R, lanes] = top
            delta_ref[b, z * R : (z + 1) * R, targets + g * LANES : targets + (g + 1) * LANES] = (
                part - top.astype(F32)
            ).astype(BF16)


def row_facts(targets, c, span, facts, firsts, ends):
    row = lax.broadcasted_iota(jnp.int32, (span, targets), 0) + c * span
    hot = jnp.where((firsts <= row) & (row < ends), 1.0, 0.0).astype(BF16)
    here = lax.dot_general(facts, hot, CONTRACT, preferred_element_type=F32).astype(jnp.int32)
    place = lax.broadcasted_iota(jnp.int32, (1, span), 1) + c * span
    rank = place - (here[2 * RT + 2 : 2 * RT + 3] * LANES + here[2 * RT + 3 : 2 * RT + 4])
    mine = lax.broadcasted_iota(jnp.int32, (RT, span), 0) == rank
    p1 = jnp.sum(jnp.where(mine, here[:RT], 0), axis=0, keepdims=True)
    p2 = jnp.sum(jnp.where(mine, here[RT : 2 * RT], 0), axis=0, keepdims=True)
    h1 = here[2 * RT : 2 * RT + 1] * WIDTH + p1
    h2 = here[2 * RT + 1 : 2 * RT + 2] * WIDTH + p2
    points = jnp.concatenate([h1, h2], axis=0)
    angle = ((8 * points) & (GRID - 1)).astype(F32) * (1.0 / GRID)
    cosines, sines = exact_turn(angle - jnp.where(angle > 0.5, 1.0, 0.0))
    c1 = (2.0 + sines[0:1] * sines[1:2]) * (1.0 / 16)
    c2 = (2.0 + cosines[0:1] * cosines[1:2]) * (1.0 / 16)
    return hot, jnp.concatenate([points.astype(F32), c1, c2], axis=0)


def skeleton_rows(own_boxes, boxes, span, hot, point, delta_ref, offs):
    twice = jnp.concatenate([hot, hot], axis=1)
    h1, h2 = point[0:1].astype(jnp.int32), point[1:2].astype(jnp.int32)
    c1, c2 = point[2:3], point[3:4]
    turn1 = point[0:1] * (1.0 / GRID) * offs
    turn1 = turn1 - jnp.floor(turn1)
    turn2 = point[1:2] * (1.0 / GRID) * offs
    turn2 = turn2 - jnp.floor(turn2)
    first = c1 * (corner(own_boxes, 0)[0].astype(F32) + offs)
    first = first * first
    block = delta_ref[boxes[0] : boxes[-1] + 1].reshape(len(boxes) * 2 * R, twice.shape[1])
    picked = lax.dot_general(block, twice, CONTRACT, preferred_element_type=F32)
    sums = []
    for n, b in enumerate(boxes):
        k1, k2 = corner(own_boxes, b)
        at = 2 * R * n
        wr, wi = picked[at : at + R], picked[at + R : at + 2 * R]
        whole = ((h1 * k1 + h2 * k2) & (GRID - 1)).astype(F32) * (1.0 / GRID)
        second = c2 * (k2.astype(F32) + offs)
        second = second * second
        phase = root(outer(first, second)) + outer(turn1, turn2 + whole)
        cosine, sine = half_turn(phase)
        real = wr * cosine - wi * sine
        imag = wr * sine + wi * cosine
        sums.append((jnp.sum(real.reshape(Q, Q, span), axis=0), jnp.sum(imag.reshape(Q, Q, span), axis=0)))
    return jnp.concatenate(
        [
            jnp.sum(sums[n][z] + sums[n + 1][z], axis=0, keepdims=True)
            for z in range(2)
            for n in range(0, len(boxes), 2)
        ],
        axis=0,
    )


def kernel(
    own_boxes, targets, parents, devices, depth,
    weights_hbm, pivots_hbm, ranks_hbm, owner_hbm, table_hbm, centre_hbm, offset_hbm, out_ref,
    weights, table, centre, offset, ranks_row, owner_row, all_pivots, delta, begin_row, stop_row, chunk_row, chunks,
    hots, points, compact, places, rows, got, mixed,
    weights_sem, const_sem, begin_sem, pivot_send, pivot_recv, rows_send, rows_recv,
):
    me = lax.axis_index("grp") * depth + lax.axis_index("dev")
    span = 2 * LANES
    spans = targets * RMEAN // span

    def device(index):
        return (lax.div(index, depth), lax.rem(index, depth))

    barrier = pltpu.get_barrier_semaphore()

    def greet(j, carry):
        pl.semaphore_signal(
            barrier, inc=1, device_id=device(lax.rem(me + j, devices)), device_id_type=pl.DeviceIdType.MESH
        )
        return carry

    pairs = [
        (ranks_hbm, ranks_row),
        (owner_hbm, owner_row),
        (table_hbm, table),
        (centre_hbm, centre),
        (offset_hbm, offset),
        (pivots_hbm, all_pivots.at[me]),
    ]
    consts = [pltpu.make_async_copy(far, near, const_sem.at[n]) for n, (far, near) in enumerate(pairs)]
    loads = [
        pltpu.make_async_copy(weights_hbm.at[:, b], weights.at[:, b], weights_sem.at[b]) for b in range(own_boxes)
    ]
    for copy in consts + loads:
        copy.start()
    lax.fori_loop(1, devices, greet, 0)
    for copy in consts:
        copy.wait()

    ranks = ranks_row[...]
    owners = owner_row[...]
    rank_down = jnp.broadcast_to(ranks, (targets, targets)).T
    owner_down = jnp.broadcast_to(owners, (targets, targets)).T
    slots = lax.broadcasted_iota(jnp.int32, (1, targets), 1)
    firsts = jnp.sum(jnp.where(owner_down < owners, rank_down, 0), axis=0, keepdims=True)
    ends = firsts + ranks
    begins = jnp.sum(jnp.where(owner_down < slots, rank_down, 0), axis=0, keepdims=True)
    begin_row[...] = begins
    stop_row[...] = jnp.sum(jnp.where(owner_down <= slots, rank_down, 0), axis=0, keepdims=True)
    chunk_row[...] = jnp.minimum(begins // LANES, 2 * spans - 1)
    to_scalars = pltpu.make_async_copy(chunk_row, chunks, begin_sem)
    to_scalars.start()

    def pivot_copy(target, source):
        return pltpu.make_async_remote_copy(
            src_ref=pivots_hbm,
            dst_ref=all_pivots.at[source],
            send_sem=pivot_send,
            recv_sem=pivot_recv,
            device_id=device(target),
            device_id_type=pl.DeviceIdType.MESH,
        )

    def send_pivots(j, carry):
        pivot_copy(lax.rem(me + j, devices), me).start()
        return carry

    def one_box(b, carry):
        pltpu.make_async_copy(weights_hbm.at[:, b], weights.at[:, b], weights_sem.at[b]).wait()
        source_box(own_boxes, targets, parents, b, weights, table, centre, offset, delta)
        return carry

    lax.fori_loop(0, 2, one_box, 0, unroll=2)
    pl.semaphore_wait(barrier, devices - 1)
    lax.fori_loop(1, devices, send_pivots, 0)
    lax.fori_loop(2, own_boxes, one_box, 0, unroll=2)

    boxes = LANES // RT
    groups = targets // devices // boxes
    tall = own_boxes // 2
    down = lax.broadcasted_iota(jnp.int32, (tall * groups, LANES), 0)
    lane = lax.broadcasted_iota(jnp.int32, (tall * groups, LANES), 1)
    opening = (down // tall) * boxes
    slot_here = opening + lane // RT
    per_tile = LANES // (groups * boxes)

    def one_tile(n, carry):
        for m in range(per_tile):
            spot = pl.ds(pl.multiple_of(n * LANES, LANES), LANES)
            first = jnp.broadcast_to(begin_row[:, spot], lane.shape)
            last = jnp.broadcast_to(stop_row[:, spot], lane.shape)
            tile_slot = slot_here + m * groups * boxes
            low = jnp.take_along_axis(first, tile_slot, axis=1, mode="promise_in_bounds")
            high = jnp.take_along_axis(last, tile_slot, axis=1, mode="promise_in_bounds")
            start = jnp.take_along_axis(first, opening + m * groups * boxes, axis=1, mode="promise_in_bounds")
            index = low + (lane & (RT - 1))
            places[n * per_tile + m] = jnp.where(index < high, index - (start & -LANES), -1)
        return carry

    lax.fori_loop(0, targets // LANES, one_tile, 0)
    to_scalars.wait()

    def drain(block, send, receive):
        copy = pltpu.make_async_remote_copy(
            src_ref=block,
            dst_ref=block,
            send_sem=send,
            recv_sem=receive,
            device_id=device(lax.rem(me + 1, devices)),
            device_id_type=pl.DeviceIdType.MESH,
        )
        copy.wait_send()
        copy.wait_recv()

    others = pl.ds(0, devices - 1)
    drain(all_pivots.at[others], pivot_send, pivot_recv)
    columns = all_pivots[...].reshape(targets, RT).astype(F32).T.astype(jnp.int32)
    facts = jnp.concatenate(
        [columns // WIDTH, columns % WIDTH, slots // COLS, slots % COLS, firsts // LANES, firsts % LANES]
        + [jnp.zeros((12, targets), jnp.int32)],
        axis=0,
    )
    facts = facts.astype(F32).astype(BF16)
    offs = offset[2 * Q : 3 * Q]
    offs = jnp.concatenate([offs, offs], axis=1)

    def one_fact(c, carry):
        hot, point = row_facts(targets, c, span, facts, firsts, ends)
        hots[c] = hot
        points[c, 0:4] = point
        return carry

    lax.fori_loop(0, spans, one_fact, 0, unroll=5 if spans % 5 == 0 else 1)
    compact[2 * spans] = jnp.zeros((tall * groups, LANES), F32)

    def rows_copy(half, target, source):
        return pltpu.make_async_remote_copy(
            src_ref=rows.at[half, target],
            dst_ref=got.at[half, source],
            send_sem=rows_send,
            recv_sem=rows_recv,
            device_id=device(target),
            device_id_type=pl.DeviceIdType.MESH,
        )

    for half in range(2):
        mine = range(half * own_boxes // 2, (half + 1) * own_boxes // 2)

        def one_span(c, carry):
            block = skeleton_rows(own_boxes, mine, span, hots[c], points[c], delta, offs)
            block = jnp.concatenate([block] * groups, axis=0)
            compact[2 * c] = block[:, :LANES]
            compact[2 * c + 1] = block[:, LANES:]
            return carry

        def place_rows(owner, carry):
            slot = owner * groups * boxes
            near, far = compact[chunks[0, slot]], compact[chunks[0, slot] + 1]
            for n in range(1, groups):
                chunk = chunks[0, slot + n * boxes]
                near = jnp.where(down >= n * tall, compact[chunk], near)
                far = jnp.where(down >= n * tall, compact[chunk + 1], far)
            place = places[owner]
            within = place & (LANES - 1)
            near = jnp.take_along_axis(near, within, axis=1, mode="promise_in_bounds")
            far = jnp.take_along_axis(far, within, axis=1, mode="promise_in_bounds")
            rows[half, owner] = jnp.where(place < 0, 0.0, jnp.where(place >= LANES, far, near))
            return carry

        def send_rows(j, carry):
            rows_copy(half, lax.rem(me + j, devices), me).start()
            return carry

        lax.fori_loop(0, spans, one_span, 0, unroll=2)
        lax.fori_loop(0, devices, place_rows, 0, unroll=8)
        lax.fori_loop(1, devices, send_rows, 0)
        got[half, me] = rows[half, me]

    drain(got.at[:, others], rows_send, rows_recv)

    pair = ROW // own_boxes
    few = own_boxes // 4

    def mix(n, carry):
        sums = []
        for k in (2 * n, 2 * n + 1):
            upper = lax.div(k, pair) * 2 * pair + lax.rem(k, pair)
            sums += [got[half, upper] + got[half, upper + pair] for half in range(2)]
        for part in range(2 * groups):
            lines = slice(part * few, (part + 1) * few)
            mixed[part, pl.ds(pl.multiple_of(n * 4 * few, 4 * few), 4 * few)] = jnp.concatenate(
                [block[lines] for block in sums], axis=0
            )
        return carry

    lax.fori_loop(0, devices // 4, mix, 0, unroll=4)
    for n in range(groups):
        for z in range(2):
            turned = mixed[2 * n + z].T
            for k in range(boxes):
                out_ref[z, :, n * boxes + k, :] = turned[k * RT : (k + 1) * RT]


def local(child_weights, pivots, ranks, owner_slot):
    depth = lax.axis_size("dev")
    devices = lax.axis_size("grp") * depth
    own_boxes = child_weights.shape[1]
    parents = child_weights.shape[4]
    targets = ranks.shape[0]
    groups = targets // devices * RT // LANES
    tall = own_boxes // 2 * groups
    sources = devices * own_boxes // 4
    spans = targets * RMEAN // (2 * LANES)
    anywhere = pl.BlockSpec(memory_space=pl.ANY)
    table, centre, offs = split_table(), centre_rows(targets), offset_columns()
    dma = pltpu.SemaphoreType.DMA
    return pl.pallas_call(
        lambda *refs: kernel(own_boxes, targets, parents, devices, depth, *refs),
        in_specs=[anywhere] * 7,
        out_specs=pl.BlockSpec(memory_space=pltpu.VMEM),
        out_shape=jax.ShapeDtypeStruct((2, RT, targets // devices, sources), F32),
        scratch_shapes=[
            pltpu.VMEM(child_weights.shape, F32),
            pltpu.VMEM(table.shape, BF16),
            pltpu.VMEM(centre.shape, F32),
            pltpu.VMEM(offs.shape, F32),
            pltpu.VMEM((1, targets), jnp.int32),
            pltpu.VMEM((1, targets), jnp.int32),
            pltpu.VMEM((devices,) + pivots.shape, jnp.int32),
            pltpu.VMEM((own_boxes, 2 * R, 2 * targets), BF16),
            pltpu.VMEM((1, targets), jnp.int32),
            pltpu.VMEM((1, targets), jnp.int32),
            pltpu.VMEM((1, targets), jnp.int32),
            pltpu.SMEM((1, targets), jnp.int32),
            pltpu.VMEM((spans, 2 * LANES, targets), BF16),
            pltpu.VMEM((spans, 8, 2 * LANES), F32),
            pltpu.VMEM((2 * spans + 1, tall, LANES), F32),
            pltpu.VMEM((devices, tall, LANES), jnp.int32),
            pltpu.VMEM((2, devices, tall, LANES), F32),
            pltpu.VMEM((2, devices, tall, LANES), F32),
            pltpu.VMEM((2 * groups, sources, LANES), F32),
            dma((own_boxes,)),
            dma((6,)),
            dma,
            dma,
            dma,
            dma,
            dma,
        ],
        compiler_params=pltpu.CompilerParams(
            collective_id=0, has_side_effects=True, vmem_limit_bytes=60 << 20
        ),
    )(child_weights, pivots, ranks.reshape(1, targets), owner_slot.reshape(1, targets), table, centre, offs)


def solution(mesh):
    in_specs = (P(None, ("grp", "dev"), None, None, None), P(("grp", "dev"), None), P(), P())
    out_specs = P(None, None, ("grp", "dev"), None)
    return jax.shard_map(local, mesh=mesh, in_specs=in_specs, out_specs=out_specs, check_vma=False)
```

```python
import math

import jax
import jax.numpy as jnp
import numpy as np
from jax import lax
from jax.experimental import pallas as pl
from jax.experimental.pallas import tpu as pltpu
from jax.sharding import PartitionSpec as P

GRID = 2048
Q = 8
RT = 32
RMEAN = 10
SIDE = GRID // 32
WIDTH = GRID // 64
ROW = GRID // 64
COLS = GRID // 32
LANES = 128
WHOLE = 1.5 * 2**23
R = Q * Q

SIN = (4.442867904603554, -7.30744348201647, 3.594788644821573, -0.7843755040132807)
COS = (1.414204082132758, -6.977642209183305, 5.715240371096478, -1.7283548501332477)
FINE_SIN = (4.442882938082702, -7.308249478180419, 3.6064755519164122, -0.8474705853915653, 0.1160367907993074, -0.009939639006380334)
FINE_COS = (1.4142135623720344, -6.97886419922267, 5.739885708281956, -1.8883460761614363, 0.3328004285822709, -0.03645323263485946, 0.002602159860467781)

F32 = jnp.float32
BF16 = jnp.bfloat16
CONTRACT = (((1,), (1,)), ((), ()))


def nodes():
    return np.cos(np.pi * (2.0 * np.arange(Q) + 1.0) / (2.0 * Q))


def lagrange(at, points):
    out = np.ones((Q, Q))
    for t in range(Q):
        for k in range(Q):
            if k != t:
                out[t] *= (points - at[k]) / (at[t] - at[k])
    return out


def child_table():
    c = nodes()
    halves = np.stack([lagrange(c, u - 0.5 + 0.5 * c) for u in (0.0, 1.0)])
    return np.einsum("uaj,vbk->abuvjk", halves, halves).reshape(R, 4 * R)


def split_table():
    table = child_table().astype(np.float32)
    high = table.astype(jnp.bfloat16)
    low = (table - high.astype(np.float32)).astype(jnp.bfloat16)
    return np.concatenate([high, low], axis=0)


def offsets():
    c = nodes()
    parent = SIDE / 2 - 0.5 + SIDE / 2 * c
    child = np.concatenate([SIDE * u / 2 + SIDE / 4 - 0.5 + SIDE / 4 * c for u in (0, 1)])
    return child, parent


def centre_rows(targets):
    a = np.arange(targets)
    x1 = (2 * WIDTH * (a // COLS) + WIDTH - 1) / (2 * GRID)
    x2 = (2 * WIDTH * (a % COLS) + WIDTH - 1) / (2 * GRID)
    c1 = (2 + np.sin(16 * np.pi * x1) * np.sin(16 * np.pi * x2)) / 16
    c2 = (2 + np.cos(16 * np.pi * x1) * np.cos(16 * np.pi * x2)) / 16
    child, parent = offsets()
    rows = [np.stack([c1, c2] + [np.zeros(targets)] * 6)]
    for o in (child, parent):
        for x in (x1, x2):
            turn = o[:, None] * x[None, :]
            rows.append(turn - np.floor(turn))
    return np.concatenate(rows).astype(np.float32)


def offset_columns():
    child, parent = offsets()
    return np.broadcast_to(np.concatenate([child, parent])[:, None], (3 * Q, LANES)).astype(np.float32)


def half_turn(phase):
    r = phase - ((phase + WHOLE) - WHOLE)
    q = r * r
    s = SIN[3]
    for coefficient in SIN[2::-1]:
        s = s * q + coefficient
    s = s * r
    c = COS[3]
    for coefficient in COS[2::-1]:
        c = c * q + coefficient
    return 1.0 - s * s, s * c


def exact_turn(r):
    q = r * r
    s, c = FINE_SIN[-1], FINE_COS[-1]
    for coefficient in FINE_SIN[-2::-1]:
        s = s * q + coefficient
    for coefficient in FINE_COS[-2::-1]:
        c = c * q + coefficient
    s = s * r
    return jnp.where(s * s < 1.0, 1.0 - s * s, c * c - 1.0), s * c


def root(square):
    return square * lax.rsqrt(square)


def corner(own_boxes, box):
    position = lax.axis_index("grp") * lax.axis_size("dev") + lax.axis_index("dev")
    box_id = position * own_boxes + box
    return (box_id // ROW) * SIDE - GRID // 2, (box_id % ROW) * SIDE - GRID // 2


def outer(column, tile):
    return jnp.concatenate([column[j : j + 1] + tile for j in range(Q)], axis=0)


def source_box(own_boxes, targets, parents, b, weights_ref, table_ref, centre_ref, offset_ref, delta_ref):
    k1, k2 = corner(own_boxes, b)
    k1f, k2f = k1.astype(F32), k2.astype(F32)
    offs = offset_ref[...]
    for g in range(targets // LANES):
        lanes = slice(g * LANES, (g + 1) * LANES)
        lane = lax.broadcasted_iota(jnp.int32, (1, LANES), 1)
        box = lane + g * LANES
        h1 = 2 * WIDTH * (box // COLS) + WIDTH - 1
        h2 = 2 * WIDTH * (box % COLS) + WIDTH - 1
        whole = ((h1 * k1 + h2 * k2) & (2 * GRID - 1)).astype(F32) * (1.0 / (2 * GRID))
        c1 = centre_ref[0:1, lanes]
        c2 = centre_ref[1:2, lanes]
        first = c1 * (k1f + offs)
        first = first * first
        second = c2 * (k2f + offs)
        second = second * second
        turn1 = centre_ref[8 : 8 + 2 * Q, lanes]
        turn2 = centre_ref[8 + 2 * Q : 8 + 4 * Q, lanes] + whole
        back1 = centre_ref[8 + 4 * Q : 8 + 5 * Q, lanes]
        back2 = centre_ref[8 + 5 * Q : 8 + 6 * Q, lanes] + whole
        parent_lane = (g * (COLS // 2)) % LANES + (lane % COLS) // 2
        pick = jnp.broadcast_to(parent_lane, (R, LANES))
        start = (g * (COLS // 2)) // LANES * LANES
        high, low = [], []
        for u in range(2):
            for v in range(2):
                one, two = slice(u * Q, (u + 1) * Q), slice(v * Q, (v + 1) * Q)
                phase = root(outer(first[one], second[two])) + outer(turn1[one], turn2[two])
                cosine, sine = half_turn(phase)
                spread = []
                for z in range(2):
                    w = weights_ref[z, b, 2 * u + v, :, start : min(start + LANES, parents)]
                    if w.shape[1] < LANES:
                        w = jnp.concatenate([w] * (LANES // w.shape[1]), axis=1)
                    spread.append(jnp.take_along_axis(w, pick, axis=1, mode="promise_in_bounds"))
                wr, wi = spread
                both = jnp.concatenate([wr * cosine + wi * sine, wi * cosine - wr * sine], axis=1)
                top = both.astype(BF16)
                high.append(top)
                low.append((both - top.astype(F32)).astype(BF16))
        wide = jnp.dot(table_ref[...], jnp.concatenate(high, axis=0), preferred_element_type=F32)
        fine = jnp.dot(table_ref[:R], jnp.concatenate(low, axis=0), preferred_element_type=F32)
        interp = wide[:R] + (wide[R:] + fine)
        ir, ii = interp[:, :LANES], interp[:, LANES:]
        parent = slice(2 * Q, 3 * Q)
        phase = root(outer(first[parent], second[parent])) + outer(back1, back2)
        cosine, sine = half_turn(phase)
        for z, part in enumerate((ir * cosine - ii * sine, ii * cosine + ir * sine)):
            top = part.astype(BF16)
            delta_ref[b, z * R : (z + 1) * R, lanes] = top
            delta_ref[b, z * R : (z + 1) * R, targets + g * LANES : targets + (g + 1) * LANES] = (
                part - top.astype(F32)
            ).astype(BF16)


def row_facts(targets, c, span, facts, firsts, ends):
    row = lax.broadcasted_iota(jnp.int32, (span, targets), 0) + c * span
    hot = jnp.where((firsts <= row) & (row < ends), 1.0, 0.0).astype(BF16)
    here = lax.dot_general(facts, hot, CONTRACT, preferred_element_type=F32).astype(jnp.int32)
    place = lax.broadcasted_iota(jnp.int32, (1, span), 1) + c * span
    rank = place - (here[2 * RT + 2 : 2 * RT + 3] * LANES + here[2 * RT + 3 : 2 * RT + 4])
    mine = lax.broadcasted_iota(jnp.int32, (RT, span), 0) == rank
    p1 = jnp.sum(jnp.where(mine, here[:RT], 0), axis=0, keepdims=True)
    p2 = jnp.sum(jnp.where(mine, here[RT : 2 * RT], 0), axis=0, keepdims=True)
    h1 = here[2 * RT : 2 * RT + 1] * WIDTH + p1
    h2 = here[2 * RT + 1 : 2 * RT + 2] * WIDTH + p2
    points = jnp.concatenate([h1, h2], axis=0)
    angle = ((8 * points) & (GRID - 1)).astype(F32) * (1.0 / GRID)
    cosines, sines = exact_turn(angle - jnp.where(angle > 0.5, 1.0, 0.0))
    c1 = (2.0 + sines[0:1] * sines[1:2]) * (1.0 / 16)
    c2 = (2.0 + cosines[0:1] * cosines[1:2]) * (1.0 / 16)
    return hot, jnp.concatenate([points.astype(F32), c1, c2], axis=0)


def skeleton_rows(own_boxes, boxes, span, hot, point, delta_ref, offs):
    twice = jnp.concatenate([hot, hot], axis=1)
    h1, h2 = point[0:1].astype(jnp.int32), point[1:2].astype(jnp.int32)
    c1, c2 = point[2:3], point[3:4]
    turn1 = point[0:1] * (1.0 / GRID) * offs
    turn1 = turn1 - jnp.floor(turn1)
    turn2 = point[1:2] * (1.0 / GRID) * offs
    turn2 = turn2 - jnp.floor(turn2)
    first = c1 * (corner(own_boxes, 0)[0].astype(F32) + offs)
    first = first * first
    block = delta_ref[boxes[0] : boxes[-1] + 1].reshape(len(boxes) * 2 * R, twice.shape[1])
    picked = lax.dot_general(block, twice, CONTRACT, preferred_element_type=F32)
    sums = []
    for n, b in enumerate(boxes):
        k1, k2 = corner(own_boxes, b)
        at = 2 * R * n
        wr, wi = picked[at : at + R], picked[at + R : at + 2 * R]
        whole = ((h1 * k1 + h2 * k2) & (GRID - 1)).astype(F32) * (1.0 / GRID)
        second = c2 * (k2.astype(F32) + offs)
        second = second * second
        phase = root(outer(first, second)) + outer(turn1, turn2 + whole)
        cosine, sine = half_turn(phase)
        real = wr * cosine - wi * sine
        imag = wr * sine + wi * cosine
        sums.append((jnp.sum(real.reshape(Q, Q, span), axis=0), jnp.sum(imag.reshape(Q, Q, span), axis=0)))
    return jnp.concatenate(
        [
            jnp.sum(sums[n][z] + sums[n + 1][z], axis=0, keepdims=True)
            for z in range(2)
            for n in range(0, len(boxes), 2)
        ],
        axis=0,
    )


def kernel(
    own_boxes, targets, parents, devices, depth,
    weights_hbm, pivots_hbm, ranks_hbm, owner_hbm, table_hbm, centre_hbm, offset_hbm, out_ref,
    weights, table, centre, offset, ranks_row, owner_row, all_pivots, delta, begin_row, stop_row, chunk_row, chunks,
    hots, points, compact, places, rows, got, mixed,
    weights_sem, const_sem, begin_sem, pivot_send, pivot_recv, rows_send, rows_recv,
):
    me = lax.axis_index("grp") * depth + lax.axis_index("dev")
    span = 2 * LANES
    spans = targets * RMEAN // span

    def device(index):
        return (lax.div(index, depth), lax.rem(index, depth))

    barrier = pltpu.get_barrier_semaphore()

    def greet(j, carry):
        pl.semaphore_signal(
            barrier, inc=1, device_id=device(lax.rem(me + j, devices)), device_id_type=pl.DeviceIdType.MESH
        )
        return carry

    pairs = [
        (ranks_hbm, ranks_row),
        (owner_hbm, owner_row),
        (table_hbm, table),
        (centre_hbm, centre),
        (offset_hbm, offset),
        (pivots_hbm, all_pivots.at[me]),
    ]
    consts = [pltpu.make_async_copy(far, near, const_sem.at[n]) for n, (far, near) in enumerate(pairs)]
    loads = [
        pltpu.make_async_copy(weights_hbm.at[:, b], weights.at[:, b], weights_sem.at[b]) for b in range(own_boxes)
    ]
    for copy in consts + loads:
        copy.start()
    lax.fori_loop(1, devices, greet, 0, unroll=True)
    for copy in consts:
        copy.wait()

    ranks = ranks_row[...]
    owners = owner_row[...]
    rank_down = jnp.broadcast_to(ranks, (targets, targets)).T
    owner_down = jnp.broadcast_to(owners, (targets, targets)).T
    slots = lax.broadcasted_iota(jnp.int32, (1, targets), 1)
    firsts = jnp.sum(jnp.where(owner_down < owners, rank_down, 0), axis=0, keepdims=True)
    ends = firsts + ranks
    begins = jnp.sum(jnp.where(owner_down < slots, rank_down, 0), axis=0, keepdims=True)
    begin_row[...] = begins
    stop_row[...] = jnp.sum(jnp.where(owner_down <= slots, rank_down, 0), axis=0, keepdims=True)
    chunk_row[...] = jnp.minimum(begins // LANES, 2 * spans - 1)
    to_scalars = pltpu.make_async_copy(chunk_row, chunks, begin_sem)
    to_scalars.start()

    def pivot_copy(target, source):
        return pltpu.make_async_remote_copy(
            src_ref=pivots_hbm,
            dst_ref=all_pivots.at[source],
            send_sem=pivot_send,
            recv_sem=pivot_recv,
            device_id=device(target),
            device_id_type=pl.DeviceIdType.MESH,
        )

    def send_pivots(j, carry):
        pivot_copy(lax.rem(me + j, devices), me).start()
        return carry

    def one_box(b, carry):
        pltpu.make_async_copy(weights_hbm.at[:, b], weights.at[:, b], weights_sem.at[b]).wait()
        source_box(own_boxes, targets, parents, b, weights, table, centre, offset, delta)
        return carry

    lax.fori_loop(0, 2, one_box, 0, unroll=2)
    pl.semaphore_wait(barrier, devices - 1)
    lax.fori_loop(1, devices, send_pivots, 0, unroll=True)
    lax.fori_loop(2, own_boxes, one_box, 0, unroll=2)

    boxes = LANES // RT
    groups = targets // devices // boxes
    tall = own_boxes // 2
    down = lax.broadcasted_iota(jnp.int32, (tall * groups, LANES), 0)
    lane = lax.broadcasted_iota(jnp.int32, (tall * groups, LANES), 1)
    opening = (down // tall) * boxes
    slot_here = opening + lane // RT
    per_tile = LANES // (groups * boxes)

    def one_tile(n, carry):
        for m in range(per_tile):
            spot = pl.ds(pl.multiple_of(n * LANES, LANES), LANES)
            first = jnp.broadcast_to(begin_row[:, spot], lane.shape)
            last = jnp.broadcast_to(stop_row[:, spot], lane.shape)
            tile_slot = slot_here + m * groups * boxes
            low = jnp.take_along_axis(first, tile_slot, axis=1, mode="promise_in_bounds")
            high = jnp.take_along_axis(last, tile_slot, axis=1, mode="promise_in_bounds")
            start = jnp.take_along_axis(first, opening + m * groups * boxes, axis=1, mode="promise_in_bounds")
            index = low + (lane & (RT - 1))
            places[n * per_tile + m] = jnp.where(index < high, index - (start & -LANES), -1)
        return carry

    lax.fori_loop(0, targets // LANES, one_tile, 0)
    to_scalars.wait()

    def drain(block, send, receive):
        copy = pltpu.make_async_remote_copy(
            src_ref=block,
            dst_ref=block,
            send_sem=send,
            recv_sem=receive,
            device_id=device(lax.rem(me + 1, devices)),
            device_id_type=pl.DeviceIdType.MESH,
        )
        copy.wait_send()
        copy.wait_recv()

    others = pl.ds(0, devices - 1)
    drain(all_pivots.at[others], pivot_send, pivot_recv)
    columns = all_pivots[...].reshape(targets, RT).astype(F32).T.astype(jnp.int32)
    facts = jnp.concatenate(
        [columns // WIDTH, columns % WIDTH, slots // COLS, slots % COLS, firsts // LANES, firsts % LANES]
        + [jnp.zeros((12, targets), jnp.int32)],
        axis=0,
    )
    facts = facts.astype(F32).astype(BF16)
    offs = offset[2 * Q : 3 * Q]
    offs = jnp.concatenate([offs, offs], axis=1)

    def one_fact(c, carry):
        hot, point = row_facts(targets, c, span, facts, firsts, ends)
        hots[c] = hot
        points[c, 0:4] = point
        return carry

    lax.fori_loop(0, spans, one_fact, 0, unroll=5 if spans % 5 == 0 else 1)
    compact[2 * spans] = jnp.zeros((tall * groups, LANES), F32)

    def rows_copy(half, target, source):
        return pltpu.make_async_remote_copy(
            src_ref=rows.at[half, target],
            dst_ref=got.at[half, source],
            send_sem=rows_send,
            recv_sem=rows_recv,
            device_id=device(target),
            device_id_type=pl.DeviceIdType.MESH,
        )

    for half in range(2):
        mine = range(half * own_boxes // 2, (half + 1) * own_boxes // 2)

        def one_span(c, carry):
            block = skeleton_rows(own_boxes, mine, span, hots[c], points[c], delta, offs)
            block = jnp.concatenate([block] * groups, axis=0)
            compact[2 * c] = block[:, :LANES]
            compact[2 * c + 1] = block[:, LANES:]
            return carry

        def place_rows(owner, carry):
            slot = owner * groups * boxes
            near, far = compact[chunks[0, slot]], compact[chunks[0, slot] + 1]
            for n in range(1, groups):
                chunk = chunks[0, slot + n * boxes]
                near = jnp.where(down >= n * tall, compact[chunk], near)
                far = jnp.where(down >= n * tall, compact[chunk + 1], far)
            place = places[owner]
            within = place & (LANES - 1)
            near = jnp.take_along_axis(near, within, axis=1, mode="promise_in_bounds")
            far = jnp.take_along_axis(far, within, axis=1, mode="promise_in_bounds")
            rows[half, owner] = jnp.where(place < 0, 0.0, jnp.where(place >= LANES, far, near))
            return carry

        def send_rows(j, carry):
            rows_copy(half, lax.rem(me + j, devices), me).start()
            return carry

        lax.fori_loop(0, spans, one_span, 0, unroll=2)
        lax.fori_loop(0, devices, place_rows, 0, unroll=8)
        lax.fori_loop(1, devices, send_rows, 0, unroll=True)
        got[half, me] = rows[half, me]

    drain(got.at[:, others], rows_send, rows_recv)

    pair = ROW // own_boxes
    few = own_boxes // 4

    def mix(n, carry):
        sums = []
        for k in (2 * n, 2 * n + 1):
            upper = lax.div(k, pair) * 2 * pair + lax.rem(k, pair)
            sums += [got[half, upper] + got[half, upper + pair] for half in range(2)]
        for part in range(2 * groups):
            lines = slice(part * few, (part + 1) * few)
            mixed[part, pl.ds(pl.multiple_of(n * 4 * few, 4 * few), 4 * few)] = jnp.concatenate(
                [block[lines] for block in sums], axis=0
            )
        return carry

    lax.fori_loop(0, devices // 4, mix, 0, unroll=4)
    for n in range(groups):
        for z in range(2):
            turned = mixed[2 * n + z].T
            for k in range(boxes):
                out_ref[z, :, n * boxes + k, :] = turned[k * RT : (k + 1) * RT]


def local(child_weights, pivots, ranks, owner_slot):
    depth = lax.axis_size("dev")
    devices = lax.axis_size("grp") * depth
    own_boxes = child_weights.shape[1]
    parents = child_weights.shape[4]
    targets = ranks.shape[0]
    groups = targets // devices * RT // LANES
    tall = own_boxes // 2 * groups
    sources = devices * own_boxes // 4
    spans = targets * RMEAN // (2 * LANES)
    anywhere = pl.BlockSpec(memory_space=pl.ANY)
    table, centre, offs = split_table(), centre_rows(targets), offset_columns()
    dma = pltpu.SemaphoreType.DMA
    return pl.pallas_call(
        lambda *refs: kernel(own_boxes, targets, parents, devices, depth, *refs),
        in_specs=[anywhere] * 7,
        out_specs=pl.BlockSpec(memory_space=pltpu.VMEM),
        out_shape=jax.ShapeDtypeStruct((2, RT, targets // devices, sources), F32),
        scratch_shapes=[
            pltpu.VMEM(child_weights.shape, F32),
            pltpu.VMEM(table.shape, BF16),
            pltpu.VMEM(centre.shape, F32),
            pltpu.VMEM(offs.shape, F32),
            pltpu.VMEM((1, targets), jnp.int32),
            pltpu.VMEM((1, targets), jnp.int32),
            pltpu.VMEM((devices,) + pivots.shape, jnp.int32),
            pltpu.VMEM((own_boxes, 2 * R, 2 * targets), BF16),
            pltpu.VMEM((1, targets), jnp.int32),
            pltpu.VMEM((1, targets), jnp.int32),
            pltpu.VMEM((1, targets), jnp.int32),
            pltpu.SMEM((1, targets), jnp.int32),
            pltpu.VMEM((spans, 2 * LANES, targets), BF16),
            pltpu.VMEM((spans, 8, 2 * LANES), F32),
            pltpu.VMEM((2 * spans + 1, tall, LANES), F32),
            pltpu.VMEM((devices, tall, LANES), jnp.int32),
            pltpu.VMEM((2, devices, tall, LANES), F32),
            pltpu.VMEM((2, devices, tall, LANES), F32),
            pltpu.VMEM((2 * groups, sources, LANES), F32),
            dma((own_boxes,)),
            dma((6,)),
            dma,
            dma,
            dma,
            dma,
            dma,
        ],
        compiler_params=pltpu.CompilerParams(
            collective_id=0, has_side_effects=True, vmem_limit_bytes=60 << 20
        ),
    )(child_weights, pivots, ranks.reshape(1, targets), owner_slot.reshape(1, targets), table, centre, offs)


def solution(mesh):
    in_specs = (P(None, ("grp", "dev"), None, None, None), P(("grp", "dev"), None), P(), P())
    out_specs = P(None, None, ("grp", "dev"), None)
    return jax.shard_map(local, mesh=mesh, in_specs=in_specs, out_specs=out_specs, check_vma=False)
```
